256 devices in a mesh: seq: 32 (over z, y_hi, core), chan: 8 (over x, y_lo).
Axes of the slice: x: 4, y: 4 (y_hi: 2, y_lo: 2; y = y_hi * 2 + y_lo), z: 8, core: 2. Of those that a mesh axis runs over, the one named last changes fastest.
Arguments:
- queries: bfloat16 [4096, 4096], P('seq', 'chan'), may hold values from -6 to 6
- keys: bfloat16 [4096, 4096], P('seq', 'chan'), may hold values from -6 to 6
- values: bfloat16 [4096, 4096], P('seq', 'chan'), may hold values from -6 to 6
- filter_weight: float32 [4096, 4096], P('seq', 'chan'), may hold values from -48 to 48
- out_weight: bfloat16 [4096, 4096], P('chan', 'seq'), may hold values from -12 to 12
- cotangent: bfloat16 [4096, 4096], P('seq', 'chan'), may hold values from -6 to 6
Outputs:
- block_out: bfloat16 [4096, 4096], P('seq', 'chan')
- query_grad: bfloat16 [4096, 4096], P('seq', 'chan')
- key_grad: bfloat16 [4096, 4096], P('seq', 'chan')
- value_grad: bfloat16 [4096, 4096], P('seq', 'chan')
- filter_grad: float32 [4096, 4096], P('seq', 'chan')
- weight_grad: float32 [4096, 4096], P('chan', 'seq')
The draws below stay inside these ranges and needn't reach their ends.
All inputs are finite; a program needn't handle non-finite values.
Results may differ from the reference program's by a relative error of at most 0.02.
Values may be sent and summed in bfloat16 or wider, within the bound.
No kernel may reach another device: no remote copies, remote signals or barrier semaphores. Data moves between devices by JAX's collectives and lax.ppermute only.
A program may use at most 128 MiB of HBM per device.

```python
import math
import jax
import jax.numpy as jnp

D = 4096
LENGTH = 4096
PADDED = 8192


def draw_filter_weight(key, part):
    key = jax.random.fold_in(key, 7)
    keys_all = jax.random.split(key, 6)
    step_count = jnp.arange(LENGTH, dtype=jnp.float32)[:, None]
    share = 0.5
    coarse_estimate = jnp.clip(jax.random.normal(keys_all[5], (LENGTH, D), jnp.float32), -4.0, 4.0)
    quick = jax.random.uniform(keys_all[0], (1, D), jnp.float32) < share
    quick_rate = jnp.exp(jax.random.uniform(keys_all[1], (1, D), jnp.float32, jnp.log(1.0 / 50.0), jnp.log(1.0 / 30.0)))
    slow_rate = jnp.exp(jax.random.uniform(keys_all[2], (1, D), jnp.float32, jnp.log(0.2), jnp.log(1.2))) / LENGTH
    decay_rate = jnp.where(quick, quick_rate, slow_rate)
    marked_positions = jax.random.randint(keys_all[3], (2,), 1, LENGTH)
    dropped_entries = jax.random.uniform(keys_all[4], (2,), jnp.float32, 0.6, 0.8)
    spike_amount = jnp.where(step_count >= marked_positions[0], dropped_entries[0], 1.0) * jnp.where(step_count >= marked_positions[1], dropped_entries[1], 1.0)
    noise_level = jnp.sqrt(LENGTH * (1.0 - jnp.exp(-2.0 * decay_rate)))
    return jnp.clip(coarse_estimate * jnp.exp(-decay_rate * step_count) * spike_amount * noise_level, -48.0, 48.0)


def spiked(values, key, source, target, blocks, factor):
    owner, partner = [(jnp.arange(values.shape[dim]) // (values.shape[dim] // blocks)).reshape([-1 if axis == dim else 1 for axis in range(values.ndim)]) for dim in (source, target)]
    chosen = jax.random.permutation(key, blocks)[partner]
    strong = (owner == chosen) | (owner == (partner + blocks // 2) % blocks)
    return jnp.where(strong, factor * values, values)


def steps_of(key, extent, pieces, smallest, high):
    factor_of, own = 1.0, jax.random.fold_in(key, 6)
    for position, shards_of in pieces:
        draws = jnp.exp(jax.random.uniform(jax.random.fold_in(own, position), (shards_of,), jnp.float32, smallest / len(pieces), high / len(pieces)))
        factor_of = factor_of * jnp.repeat(draws, extent[position] // shards_of).reshape([-1 if axis == position else 1 for axis in range(len(extent))])
    return factor_of


def normal_values(stream_key, extent, deviation, reach, cuts=(), held_as=jnp.bfloat16):
    values = deviation * jax.random.normal(stream_key, extent, jnp.float32)
    if cuts:
        values = values * steps_of(stream_key, extent, cuts, -0.22, 0.18)
    return jnp.clip(values, -reach, reach).astype(held_as)


def bell_draw_with(key, shape, spread, limit, pieces, heavy, kind=jnp.bfloat16):
    values = spread * jax.random.normal(key, shape, jnp.float32)
    if pieces:
        values = values * steps_of(key, shape, pieces, -0.22, 0.18)
    return jnp.clip(spiked(values, jax.random.fold_in(key, 3), *heavy), -limit, limit).astype(kind)


def setup_inputs(seed: int = 0) -> dict:
    key_list = jax.random.split(jax.random.key(seed), 7)
    return {
        "queries": normal_values(key_list[0], (LENGTH, D), 1.0, 6.0, ((0, 32), (1, 8))),
        "keys": normal_values(key_list[1], (LENGTH, D), 1.0, 6.0, ((0, 32), (1, 8))),
        "values": normal_values(key_list[2], (LENGTH, D), 1.0, 6.0, ((0, 32), (1, 8))),
        "filter_weight": draw_filter_weight(jax.random.fold_in(key_list[6], 71), 0),
        "out_weight": bell_draw_with(key_list[4], (D, D), 1 ** -0.5, 12.0, ((0, 8), (1, 32)), (0, 1, 32, 2.75)),
        "cotangent": bell_draw_with(key_list[5], (LENGTH, D), 1.0, 6.0, ((0, 32), (1, 8)), (0, 1, 32, 2.75)),
    }


def reference(queries, keys, values, filter_weight, out_weight, cotangent):
    product = keys.astype(jnp.float32) * values.astype(jnp.float32)
    filter_scaled = filter_weight.astype(jnp.float32) / math.sqrt(LENGTH)
    product_spec = jnp.fft.rfft(product, n=PADDED, axis=0)
    filter_spec = jnp.fft.rfft(filter_scaled, n=PADDED, axis=0)
    conv = jnp.fft.irfft(product_spec * filter_spec, n=PADDED, axis=0)[:LENGTH]
    query_f = queries.astype(jnp.float32)
    mixed = (query_f * conv).astype(jnp.bfloat16)
    weight_scale = 1.0 / math.sqrt(D)
    block_out = (jnp.dot(mixed, out_weight, preferred_element_type=jnp.float32) * weight_scale).astype(jnp.bfloat16)
    mixed_grad = jnp.dot(cotangent, out_weight.T, preferred_element_type=jnp.float32) * weight_scale
    query_grad = (mixed_grad * conv).astype(jnp.bfloat16)
    conv_grad = mixed_grad * query_f
    grad_spec = jnp.fft.rfft(conv_grad, n=PADDED, axis=0)
    product_grad = jnp.fft.irfft(grad_spec * jnp.conj(filter_spec), n=PADDED, axis=0)[:LENGTH]
    filter_raw = jnp.fft.irfft(grad_spec * jnp.conj(product_spec), n=PADDED, axis=0)[:LENGTH]
    key_grad = (product_grad * values.astype(jnp.float32)).astype(jnp.bfloat16)
    value_grad = (product_grad * keys.astype(jnp.float32)).astype(jnp.bfloat16)
    filter_grad = filter_raw / math.sqrt(LENGTH)
    weight_grad = jnp.dot(mixed.T, cotangent, preferred_element_type=jnp.float32) * weight_scale
    return (block_out, query_grad, key_grad, value_grad, filter_grad, weight_grad)
```

```python
import functools
import math

import jax
import jax.numpy as jnp
import numpy as np
from jax import lax
from jax.experimental import pallas as pl
from jax.experimental.pallas import tpu as pltpu
from jax.sharding import Mesh
from jax.sharding import PartitionSpec as P

D = 4096
LENGTH = 4096
PADDED = 2 * LENGTH
LANE = 128
OUTER = PADDED // LANE
HALF = OUTER // 2
ROWS = HALF + 1
CH = 16
WIDE = 512
Z, H, K, C = 8, 2, 2, 8
SEQ = ("z", "h", "k")
PLANE = ("h", "chan")
BF = jnp.bfloat16
F32 = jnp.float32
SCALE = 1.0 / math.sqrt(D)


def halves(table):
    high = np.asarray(table, np.float32).astype(BF)
    low = (np.asarray(table, np.float64) - high.astype(np.float64)).astype(np.float32).astype(BF)
    return np.stack([high, low])


@functools.lru_cache(maxsize=1)
def make_tables():
    outer = np.arange(ROWS)[:, None] * np.arange(HALF)[None, :] % OUTER
    angle = -2.0 * np.pi / OUTER * outer
    eye = np.eye(CH)
    first = np.concatenate([np.kron(np.cos(angle), eye), np.kron(np.sin(angle), eye)], axis=0)
    inner = np.arange(LANE)[:, None] * np.arange(LANE)[None, :] % LANE
    inner_cos = np.cos(2.0 * np.pi / LANE * inner)
    inner_sin = np.sin(-2.0 * np.pi / LANE * inner)
    second = np.block([[inner_cos, inner_sin], [-inner_sin, inner_cos]])
    turn = -2.0 * np.pi / PADDED * (np.arange(ROWS)[:, None] * np.arange(LANE)[None, :])
    turn = np.repeat(turn, CH, axis=0)
    twist = np.stack([np.cos(turn), np.sin(turn)]).astype(np.float32)
    count = np.full((ROWS,), 2.0)
    count[0] = count[-1] = 1.0
    back = count[None, :] / PADDED
    last = np.concatenate(
        [np.kron(np.cos(angle).T * back, eye), np.kron(np.sin(angle).T * back, eye)], axis=1
    )
    return (halves(first), halves(second), halves(second.T), twist, halves(last))


def split(x):
    high = x.astype(BF)
    return high, (x - high.astype(F32)).astype(BF)


def dot(a, b):
    return jnp.dot(a, b, preferred_element_type=F32)


def dot3(a, table):
    high, low = split(a)
    return dot(high, table[0]) + (dot(low, table[0]) + dot(high, table[1]))


def table_dot3(table, b):
    high, low = split(b)
    return dot(table[0], high) + (dot(table[0], low) + dot(table[1], high))


N = ROWS * CH


def spread(mid, twist, col):
    real = mid[:N, col : col + LANE]
    imag = mid[N:, col : col + LANE]
    return jnp.concatenate(
        [real * twist[0] - imag * twist[1], real * twist[1] + imag * twist[0]], axis=1
    )


def unspread(mid, twist):
    real = mid[:, :LANE]
    imag = mid[:, LANE:]
    return jnp.concatenate(
        [real * twist[0] + imag * twist[1], imag * twist[0] - real * twist[1]], axis=0
    )


def times(a, b):
    ar, ai, br, bi = a[:, :LANE], a[:, LANE:], b[:, :LANE], b[:, LANE:]
    return jnp.concatenate([ar * br - ai * bi, ar * bi + ai * br], axis=1)


def times_conj(a, b):
    ar, ai, br, bi = a[:, :LANE], a[:, LANE:], b[:, :LANE], b[:, LANE:]
    return jnp.concatenate([ar * br + ai * bi, ai * br - ar * bi], axis=1)


def pack_kernel(query, key, value, weight, out):
    product = key[...].astype(F32) * value[...].astype(F32)
    signals = (product, weight[...] * (1.0 / math.sqrt(LENGTH)), query[...].astype(F32))
    for i, signal in enumerate(signals):
        rows = signal.T.astype(BF).reshape(HALF, CH, LANE)
        out[:, i * CH : (i + 1) * CH, :] = rows


def share_kernel(cot, out):
    k = lax.axis_index("k")
    for h in range(H):
        for j in range(K):
            side = pl.multiple_of((2 * h + (k + j) % 2) * LANE, LANE)
            piece = cot[:, pl.ds(side, LANE)]
            for c in range(C):
                out[h * C + c, :, j * LANE : (j + 1) * LANE] = piece


def conv_kernel(packed, first, second, second_back, twist, last, mixed, conv, spectra):
    product = packed[:, 0:CH, :].reshape(HALF * CH, LANE)
    weight = packed[:, CH : 2 * CH, :].reshape(HALF * CH, LANE)
    query = packed[:, 2 * CH :, :].reshape(HALF * CH, LANE)
    both = jnp.concatenate([product, weight], axis=1)
    mid = dot(first[0], both) + dot(first[1], both)
    spec = dot3(
        jnp.concatenate([spread(mid, twist, 0), spread(mid, twist, LANE)], axis=0), second
    )
    spectra[...] = spec
    turned = unspread(dot3(times(spec[:N], spec[N:]), second_back), twist)
    result = table_dot3(last, turned)
    conv[...] = result
    mixed[...] = (query.astype(F32) * result).astype(BF)


def grad_kernel(own, other, cot, mixed, out):
    for z in range(Z):
        for h in range(H):
            for k in range(K):
                for part in range(2):
                    a = 4 * z + 2 * part + k
                    out[4 * z + 2 * h + k, part * CH : (part + 1) * CH, :] = mixed[
                        a * CH : (a + 1) * CH, :
                    ]
    total = jnp.zeros((WIDE, H * LANE), F32)
    for z in range(Z):
        weight = jnp.concatenate([own[z], other[z]], axis=1)
        rows = jnp.concatenate([cot[h * C + z] for h in range(H)], axis=0)
        total = total + lax.dot_general(
            weight, rows, (((1,), (1,)), ((), ())), preferred_element_type=F32
        )
    total = (total * SCALE).astype(BF)
    for part in range(2):
        out[:, (2 + part) * CH : (3 + part) * CH, :] = total[
            :, part * LANE : (part + 1) * LANE
        ].reshape(HALF, CH, LANE)


def tile_of(moved):
    return jnp.concatenate(
        [moved[:, p * CH : (p + 1) * CH, :].reshape(WIDE, LANE) for p in range(2)], axis=1
    )


def project_kernel(moved, own, other, out):
    mixed = tile_of(moved).astype(F32).T.astype(BF)
    for z in range(Z):
        weight = jnp.concatenate([own[z], other[z]], axis=1)
        part = (dot(mixed, weight) * SCALE).astype(BF)
        for h in range(H):
            out[h * C + z] = part[h * LANE : (h + 1) * LANE]


def weight_kernel(moved, moved_other, cot, cot_other, out):
    mixed = jnp.concatenate([tile_of(moved), tile_of(moved_other)], axis=1)
    for z in range(0, Z, 2):
        columns = []
        for y in (z, z + 1):
            rows = [cot[h * C + y, :, :LANE] for h in range(H)]
            rows += [cot_other[h * C + y, :, LANE:] for h in range(H)]
            columns.append(jnp.concatenate(rows, axis=0))
        grad = dot(mixed, jnp.concatenate(columns, axis=1)) * SCALE
        out[z] = grad[:, :LANE].astype(out.dtype)
        out[z + 1] = grad[:, LANE:].astype(out.dtype)


def back_kernel(moved, packed, conv, spectra, first, second, second_back, twist, last, out):
    pieces = []
    for z in range(Z):
        for part in range(2):
            for k in range(K):
                low = (2 + part) * CH
                pieces.append(
                    moved[4 * z + k, low : low + CH, :].astype(F32)
                    + moved[4 * z + 2 + k, low : low + CH, :].astype(F32)
                )
    mixed_grad = jnp.concatenate(pieces, axis=0)
    query = packed[:, 2 * CH :, :].reshape(HALF * CH, LANE).astype(F32)
    query_grad = (mixed_grad * conv[...]).astype(BF)
    high, low = split(mixed_grad * query)
    sides = dot(first[0], jnp.concatenate([high, low], axis=1))
    mid = sides[:, :LANE] + (sides[:, LANE:] + dot(first[1], high))
    grad = dot3(spread(mid, twist, 0), second)
    product_spec, filter_spec = spectra[:N], spectra[N:]
    both = dot3(
        jnp.concatenate([times_conj(grad, filter_spec), times_conj(grad, product_spec)], axis=0),
        second_back,
    )
    turned = jnp.concatenate([unspread(both[:N], twist), unspread(both[N:], twist)], axis=1)
    result = table_dot3(last, turned).astype(BF)
    out[:, 0:CH, :] = result[:, :LANE].reshape(HALF, CH, LANE)
    out[:, CH : 2 * CH, :] = result[:, LANE:].reshape(HALF, CH, LANE)
    out[:, 2 * CH :, :] = query_grad.reshape(HALF, CH, LANE)


def finish_kernel(moved, key, value, query_grad, key_grad, value_grad, filter_grad):
    def turned(i):
        return moved[:, i * CH : (i + 1) * CH, :].reshape(WIDE, LANE).astype(F32).T

    product_grad = turned(0)
    key_grad[...] = (product_grad * value[...].astype(F32)).astype(BF)
    value_grad[...] = (product_grad * key[...].astype(F32)).astype(BF)
    filter_grad[...] = turned(1) * (1.0 / math.sqrt(LENGTH))
    query_grad[...] = turned(2).astype(BF)


def sum_kernel(moved, out):
    k = lax.axis_index("k")
    for h in range(H):
        total = moved[h * C].astype(F32)
        for c in range(1, C):
            total = total + moved[h * C + c].astype(F32)
        total = total.astype(BF)
        for j in range(K):
            side = pl.multiple_of((2 * h + (k + j) % 2) * LANE, LANE)
            out[:, pl.ds(side, LANE)] = total[:, j * LANE : (j + 1) * LANE]


def call(kernel, outs, *args, flops=0):
    shapes = tuple(jax.ShapeDtypeStruct(s, d) for s, d in outs)
    return pl.pallas_call(
        kernel,
        out_shape=shapes,
        in_specs=[pl.BlockSpec(memory_space=pltpu.VMEM)] * len(args),
        out_specs=tuple([pl.BlockSpec(memory_space=pltpu.VMEM)] * len(outs)),
        compiler_params=pltpu.CompilerParams(vmem_limit_bytes=60 * 1024 * 1024),
        cost_estimate=pl.CostEstimate(flops=flops, bytes_accessed=4 << 20, transcendentals=0),
        name=kernel.__name__,
    )(*args)


def exchange(x, axes):
    return lax.all_to_all(x, axes, split_axis=0, concat_axis=0, tiled=True)


def local(queries, keys, values, filter_weight, out_weight, cotangent):
    first, second, second_back, twist, last = make_tables()
    core_pair = [(0, 1), (1, 0)]
    (packed,) = call(
        pack_kernel, [((HALF, 3 * CH, LANE), BF)], queries, keys, values, filter_weight
    )
    (shared,) = call(share_kernel, [((H * C, LANE, K * LANE), BF)], cotangent)
    own = lax.all_gather(out_weight, "z")
    packed = exchange(packed, SEQ)
    packed, shared = lax.optimization_barrier((packed, shared))
    cot = exchange(shared, PLANE)
    mixed, conv, spectra = call(
        conv_kernel,
        [((HALF * CH, LANE), BF), ((HALF * CH, LANE), F32), ((2 * N, 2 * LANE), F32)],
        packed, first, second, second_back, twist, last, flops=5_000_000_000,
    )
    mixed, conv, spectra = call(
        conv_kernel,
        [((HALF * CH, LANE), BF), ((HALF * CH, LANE), F32), ((2 * N, 2 * LANE), F32)],
        packed, first, second, second_back, twist, last, flops=5_000_000_000,
    )
    own, cot = lax.optimization_barrier((own, cot))
    other = lax.ppermute(own, "k", core_pair)
    cot_other = lax.ppermute(cot, "k", core_pair)
    own, cot, mixed = lax.optimization_barrier((own, cot, mixed))
    other = lax.ppermute(own, "k", core_pair)
    cot_other = lax.ppermute(cot, "k", core_pair)
    (sent,) = call(grad_kernel, [((HALF, 4 * CH, LANE), BF)], own, other, cot, mixed)
    moved = exchange(sent, SEQ)
    moved_other = lax.ppermute(moved, "k", core_pair)
    (out_part,) = call(project_kernel, [((H * C, LANE, K * LANE), BF)], moved, own, other)
    (weight_part,) = call(
        weight_kernel, [((Z, WIDE, LANE), F32)], moved, moved_other, cot, cot_other
    )
    weight_grad = lax.psum_scatter(
        weight_part.reshape(Z * WIDE, LANE), "z", scatter_dimension=0, tiled=True
    )
    out_parts = exchange(out_part, PLANE)
    (back,) = call(
        back_kernel, [((HALF, 3 * CH, LANE), BF)],
        moved, packed, conv, spectra, first, second, second_back, twist, last, flops=8_000_000_000,
    )
    back, out_parts = lax.optimization_barrier((back, out_parts))
    back = exchange(back, SEQ)
    (block_out,) = call(sum_kernel, [((LANE, WIDE), BF)], out_parts)
    query_grad, key_grad, value_grad, filter_grad = call(
        finish_kernel,
        [((LANE, WIDE), BF), ((LANE, WIDE), BF), ((LANE, WIDE), BF), ((LANE, WIDE), F32)],
        back, keys, values,
    )
    return (block_out, query_grad, key_grad, value_grad, filter_grad, weight_grad)


def solution(mesh):
    split_mesh = Mesh(mesh.devices.reshape(Z, H, K, C), ("z", "h", "k", "chan"))
    by_position = P(SEQ, "chan")
    by_channel = P("chan", SEQ)
    in_specs = (by_position,) * 4 + (by_channel, by_position)
    out_specs = (by_position,) * 5 + (by_channel,)
    return jax.shard_map(
        local, mesh=split_mesh, in_specs=in_specs, out_specs=out_specs, check_vma=False
    )
```

```python
import functools
import math

import jax
import jax.numpy as jnp
import numpy as np
from jax import lax
from jax.experimental import pallas as pl
from jax.experimental.pallas import tpu as pltpu
from jax.sharding import Mesh
from jax.sharding import PartitionSpec as P

D = 4096
LENGTH = 4096
PADDED = 2 * LENGTH
LANE = 128
OUTER = PADDED // LANE
HALF = OUTER // 2
ROWS = HALF + 1
CH = 16
WIDE = 512
Z, H, K, C = 8, 2, 2, 8
SEQ = ("z", "h", "k")
PLANE = ("h", "chan")
BF = jnp.bfloat16
F32 = jnp.float32
SCALE = 1.0 / math.sqrt(D)
GRANT = 40 * 1024 * 1024
FULL = 64 * 1024 * 1024


def halves(table):
    high = np.asarray(table, np.float32).astype(BF)
    low = (np.asarray(table, np.float64) - high.astype(np.float64)).astype(np.float32).astype(BF)
    return np.stack([high, low])


@functools.lru_cache(maxsize=1)
def make_tables():
    outer = np.arange(ROWS)[:, None] * np.arange(HALF)[None, :] % OUTER
    angle = -2.0 * np.pi / OUTER * outer
    eye = np.eye(CH)
    first = np.concatenate([np.kron(np.cos(angle), eye), np.kron(np.sin(angle), eye)], axis=0)
    inner = np.arange(LANE)[:, None] * np.arange(LANE)[None, :] % LANE
    inner_cos = np.cos(2.0 * np.pi / LANE * inner)
    inner_sin = np.sin(-2.0 * np.pi / LANE * inner)
    second = np.block([[inner_cos, inner_sin], [-inner_sin, inner_cos]])
    turn = -2.0 * np.pi / PADDED * (np.arange(ROWS)[:, None] * np.arange(LANE)[None, :])
    turn = np.repeat(turn, CH, axis=0)
    twist = np.stack([np.cos(turn), np.sin(turn)]).astype(np.float32)
    count = np.full((ROWS,), 2.0)
    count[0] = count[-1] = 1.0
    back = count[None, :] / PADDED
    last = np.concatenate(
        [np.kron(np.cos(angle).T * back, eye), np.kron(np.sin(angle).T * back, eye)], axis=1
    )
    return (halves(first), halves(second), halves(second.T), twist, halves(last))


def split(x):
    high = x.astype(BF)
    return high, (x - high.astype(F32)).astype(BF)


def dot(a, b):
    return jnp.dot(a, b, preferred_element_type=F32)


def dot3(a, table):
    high, low = split(a)
    return dot(high, table[0]) + (dot(low, table[0]) + dot(high, table[1]))


def table_dot3(table, b):
    high, low = split(b)
    return dot(table[0], high) + (dot(table[0], low) + dot(table[1], high))


N = ROWS * CH


def spread(mid, twist, col):
    real = mid[:N, col : col + LANE]
    imag = mid[N:, col : col + LANE]
    return jnp.concatenate(
        [real * twist[0] - imag * twist[1], real * twist[1] + imag * twist[0]], axis=1
    )


def unspread(mid, twist):
    real = mid[:, :LANE]
    imag = mid[:, LANE:]
    return jnp.concatenate(
        [real * twist[0] + imag * twist[1], imag * twist[0] - real * twist[1]], axis=0
    )


def times(a, b):
    ar, ai, br, bi = a[:, :LANE], a[:, LANE:], b[:, :LANE], b[:, LANE:]
    return jnp.concatenate([ar * br - ai * bi, ar * bi + ai * br], axis=1)


def times_conj(a, b):
    ar, ai, br, bi = a[:, :LANE], a[:, LANE:], b[:, :LANE], b[:, LANE:]
    return jnp.concatenate([ar * br + ai * bi, ai * br - ar * bi], axis=1)


def pack_kernel(key, value, weight, query, out, query_t):
    product = key[...].astype(F32) * value[...].astype(F32)
    for i, signal in enumerate((product, weight[...] * (1.0 / math.sqrt(LENGTH)))):
        out[:, i * CH : (i + 1) * CH, :] = signal.T.astype(BF).reshape(HALF, CH, LANE)
    query_t[...] = query[...].astype(F32).T.astype(BF)


def share_kernel(cot, out):
    k = lax.axis_index("k")
    for h in range(H):
        for j in range(K):
            side = pl.multiple_of((2 * h + (k + j) % 2) * LANE, LANE)
            piece = cot[:, pl.ds(side, LANE)]
            for c in range(C):
                out[h * C + c, :, j * LANE : (j + 1) * LANE] = piece


def conv_kernel(packed, first, second, second_back, twist, last, conv, spectra):
    product = packed[:, 0:CH, :].reshape(HALF * CH, LANE)
    weight = packed[:, CH:, :].reshape(HALF * CH, LANE)
    both = jnp.concatenate([product, weight], axis=1)
    mid = dot(first[0], both) + dot(first[1], both)
    spec = dot3(
        jnp.concatenate([spread(mid, twist, 0), spread(mid, twist, LANE)], axis=0), second
    )
    spectra[...] = spec
    turned = unspread(dot3(times(spec[:N], spec[N:]), second_back), twist)
    conv[...] = table_dot3(last, turned).astype(BF)


def grad_kernel(own, other, cot, conv, query, query_pair, out, kept, sent):
    here = lax.axis_index("h")
    for z in range(Z):
        for h in range(H):
            for k in range(K):
                for part in range(2):
                    a = 4 * z + 2 * part + k
                    out[4 * z + 2 * h + k, part * CH : (part + 1) * CH, :] = conv[
                        a * CH : (a + 1) * CH, :
                    ]
    total = jnp.zeros((WIDE, H * LANE), F32)
    for z in range(Z):
        weight = jnp.concatenate([own[z], other[z]], axis=1)
        rows = jnp.concatenate([cot[h * C + z] for h in range(H)], axis=0)
        total = total + lax.dot_general(
            weight, rows, (((1,), (1,)), ((), ())), preferred_element_type=F32
        )
    total = total * SCALE
    left, right = total[:, :LANE], total[:, LANE:]
    kept[...] = jnp.where(here == 0, left, right)
    sent[...] = jnp.where(here == 0, right, left).astype(BF)
    for part, side in enumerate((left, right)):
        gate = jnp.where(here == part, query[...].astype(F32), query_pair[...].astype(F32))
        grad = (side * gate).astype(BF)
        out[:, (2 + part) * CH : (3 + part) * CH, :] = grad.reshape(HALF, CH, LANE)


def tile_of(moved, query, query_pair):
    here = lax.axis_index("h")
    parts = []
    for p in range(2):
        conv = moved[:, p * CH : (p + 1) * CH, :].reshape(WIDE, LANE).astype(F32)
        gate = jnp.where(here == p, query[...].astype(F32), query_pair[...].astype(F32))
        parts.append((gate * conv).astype(BF))
    return jnp.concatenate(parts, axis=1)


def project_kernel(moved, query, query_pair, own, other, out):
    mixed = tile_of(moved, query, query_pair).astype(F32).T.astype(BF)
    for z in range(Z):
        weight = jnp.concatenate([own[z], other[z]], axis=1)
        part = (dot(mixed, weight) * SCALE).astype(BF)
        for h in range(H):
            out[h * C + z] = part[h * LANE : (h + 1) * LANE]


def weight_kernel(moved, moved_other, query, pair, query_other, pair_other, cot, cot_other, out):
    mixed = jnp.concatenate(
        [tile_of(moved, query, pair), tile_of(moved_other, query_other, pair_other)], axis=1
    )
    for z in range(0, Z, 2):
        columns = []
        for y in (z, z + 1):
            rows = [cot[h * C + y, :, :LANE] for h in range(H)]
            rows += [cot_other[h * C + y, :, LANE:] for h in range(H)]
            columns.append(jnp.concatenate(rows, axis=0))
        grad = dot(mixed, jnp.concatenate(columns, axis=1)) * SCALE
        out[z] = grad[:, :LANE].astype(out.dtype)
        out[z + 1] = grad[:, LANE:].astype(out.dtype)


def back_kernel(moved, spectra, first, second, second_back, twist, last, out):
    pieces = []
    for z in range(Z):
        for part in range(2):
            for k in range(K):
                low = (2 + part) * CH
                pieces.append(
                    moved[4 * z + k, low : low + CH, :].astype(F32)
                    + moved[4 * z + 2 + k, low : low + CH, :].astype(F32)
                )
    high, low = split(jnp.concatenate(pieces, axis=0))
    sides = dot(first[0], jnp.concatenate([high, low], axis=1))
    mid = sides[:, :LANE] + (sides[:, LANE:] + dot(first[1], high))
    grad = dot3(spread(mid, twist, 0), second)
    product_spec, filter_spec = spectra[:N], spectra[N:]
    both = dot3(
        jnp.concatenate([times_conj(grad, filter_spec), times_conj(grad, product_spec)], axis=0),
        second_back,
    )
    turned = jnp.concatenate([unspread(both[:N], twist), unspread(both[N:], twist)], axis=1)
    result = table_dot3(last, turned).astype(BF)
    out[:, 0:CH, :] = result[:, :LANE].reshape(HALF, CH, LANE)
    out[:, CH:, :] = result[:, LANE:].reshape(HALF, CH, LANE)


def finish_kernel(moved, key, value, key_grad, value_grad, filter_grad):
    def turned(i):
        return moved[:, i * CH : (i + 1) * CH, :].reshape(WIDE, LANE).astype(F32).T

    product_grad = turned(0)
    key_grad[...] = (product_grad * value[...].astype(F32)).astype(BF)
    value_grad[...] = (product_grad * key[...].astype(F32)).astype(BF)
    filter_grad[...] = turned(1) * (1.0 / math.sqrt(LENGTH))


def sum_kernel(parts, moved, kept, received, out, query_grad):
    k = lax.axis_index("k")
    for h in range(H):
        total = parts[h * C].astype(F32)
        for c in range(1, C):
            total = total + parts[h * C + c].astype(F32)
        total = total.astype(BF)
        for j in range(K):
            side = pl.multiple_of((2 * h + (k + j) % 2) * LANE, LANE)
            out[:, pl.ds(side, LANE)] = total[:, j * LANE : (j + 1) * LANE]
    left = moved[:, 0:CH, :].reshape(WIDE, LANE).astype(F32)
    right = moved[:, CH : 2 * CH, :].reshape(WIDE, LANE).astype(F32)
    conv = jnp.where(lax.axis_index("h") == 0, left, right)
    grad = (kept[...] + received[...].astype(F32)) * conv
    query_grad[...] = grad.T.astype(BF)


class Late:
    def __init__(self, ref, buffer, semaphore):
        self.buffer, self.copy, self.waiting = buffer, pltpu.make_async_copy(ref, buffer, semaphore), True
        self.copy.start()

    def __getitem__(self, index):
        if self.waiting:
            self.copy.wait()
            self.waiting = False
        return self.buffer[index]


def call(kernel, outs, *args, flops=0, late=(), grant=GRANT):
    shapes = tuple(jax.ShapeDtypeStruct(s, d) for s, d in outs)

    def body(*refs):
        refs = list(refs)
        if late:
            semaphores = refs.pop()
            buffers = refs[len(args) + len(outs) :]
            refs = refs[: len(args) + len(outs)]
            for i, at in enumerate(late):
                refs[at] = Late(refs[at], buffers[i], semaphores.at[i])
        kernel(*refs)
        for at in late:
            if refs[at].waiting:
                refs[at].copy.wait()

    scratch = [pltpu.VMEM(args[at].shape, args[at].dtype) for at in late]
    if late:
        scratch.append(pltpu.SemaphoreType.DMA((len(late),)))
    return pl.pallas_call(
        body,
        out_shape=shapes,
        in_specs=[
            pl.BlockSpec(memory_space=pltpu.HBM if i in late else pltpu.VMEM)
            for i in range(len(args))
        ],
        out_specs=tuple([pl.BlockSpec(memory_space=pltpu.VMEM)] * len(outs)),
        scratch_shapes=scratch,
        compiler_params=pltpu.CompilerParams(vmem_limit_bytes=grant),
        cost_estimate=pl.CostEstimate(flops=flops, bytes_accessed=4 << 20, transcendentals=0),
        name=kernel.__name__,
    )(*args)


def exchange(x, axes):
    return lax.all_to_all(x, axes, split_axis=0, concat_axis=0, tiled=True)


def local(queries, keys, values, filter_weight, out_weight, cotangent):
    first, second, second_back, twist, last = make_tables()
    core_pair = [(0, 1), (1, 0)]
    packed, query_t = call(
        pack_kernel,
        [((HALF, 2 * CH, LANE), BF), ((WIDE, LANE), BF)],
        keys, values, filter_weight, queries, late=(0, 1, 2, 3), grant=FULL,
    )
    (shared,) = call(share_kernel, [((H * C, LANE, K * LANE), BF)], cotangent)
    query = (query_t, lax.ppermute(query_t, "h", core_pair))
    own = lax.all_gather(out_weight, "z")
    packed = exchange(packed, SEQ)
    packed, shared, query = lax.optimization_barrier((packed, shared, query))
    query_other = tuple(lax.ppermute(side, "k", core_pair) for side in query)
    cot = exchange(shared, PLANE)
    conv, spectra = call(
        conv_kernel,
        [((HALF * CH, LANE), BF), ((2 * N, 2 * LANE), F32)],
        packed, first, second, second_back, twist, last, flops=5_000_000_000, late=(1, 2, 3, 4, 5),
    )
    own, cot, conv = lax.optimization_barrier((own, cot, conv))
    other = lax.ppermute(own, "k", core_pair)
    cot_other = lax.ppermute(cot, "k", core_pair)
    sent, kept, passed = call(
        grad_kernel,
        [((HALF, 4 * CH, LANE), BF), ((WIDE, LANE), F32), ((WIDE, LANE), BF)],
        own, other, cot, conv, *query,
    )
    received = lax.ppermute(passed, "h", core_pair)
    moved = exchange(sent, SEQ)
    moved_other = lax.ppermute(moved, "k", core_pair)
    (out_part,) = call(project_kernel, [((H * C, LANE, K * LANE), BF)], moved, *query, own, other)
    moved_other, _ = lax.optimization_barrier((moved_other, out_part))
    (weight_part,) = call(
        weight_kernel,
        [((Z, WIDE, LANE), F32)],
        moved, moved_other, *query, *query_other, cot, cot_other,
    )
    weight_grad = lax.psum_scatter(
        weight_part.reshape(Z * WIDE, LANE), "z", scatter_dimension=0, tiled=True
    )
    out_parts = exchange(out_part, PLANE)
    (back,) = call(
        back_kernel, [((HALF, 2 * CH, LANE), BF)],
        moved, spectra, first, second, second_back, twist, last, flops=8_000_000_000,
        late=(1, 2, 3, 4, 5, 6),
    )
    back, out_parts = lax.optimization_barrier((back, out_parts))
    back = exchange(back, SEQ)
    block_out, query_grad = call(
        sum_kernel,
        [((LANE, WIDE), BF), ((LANE, WIDE), BF)],
        out_parts, moved, kept, received,
    )
    key_grad, value_grad, filter_grad = call(
        finish_kernel,
        [((LANE, WIDE), BF), ((LANE, WIDE), BF), ((LANE, WIDE), F32)],
        back, keys, values,
    )
    return (block_out, query_grad, key_grad, value_grad, filter_grad, weight_grad)


def solution(mesh):
    split_mesh = Mesh(mesh.devices.reshape(Z, H, K, C), ("z", "h", "k", "chan"))
    by_position = P(SEQ, "chan")
    by_channel = P("chan", SEQ)
    in_specs = (by_position,) * 4 + (by_channel, by_position)
    out_specs = (by_position,) * 5 + (by_channel,)
    return jax.shard_map(
        local, mesh=split_mesh, in_specs=in_specs, out_specs=out_specs, check_vma=False
    )
```

```python
import functools
import math

import jax
import jax.numpy as jnp
import numpy as np
from jax import lax
from jax.experimental import pallas as pl
from jax.experimental.pallas import tpu as pltpu
from jax.sharding import Mesh
from jax.sharding import PartitionSpec as P

D = 4096
LENGTH = 4096
PADDED = 2 * LENGTH
LANE = 128
OUTER = PADDED // LANE
HALF = OUTER // 2
ROWS = HALF + 1
CH = 16
WIDE = 512
Z, H, K, C = 8, 2, 2, 8
SEQ = ("z", "h", "k")
PLANE = ("h", "chan")
BF = jnp.bfloat16
F32 = jnp.float32
SCALE = 1.0 / math.sqrt(D)
GRANT = 40 * 1024 * 1024
FULL = 64 * 1024 * 1024


def halves(table):
    high = np.asarray(table, np.float32).astype(BF)
    low = (np.asarray(table, np.float64) - high.astype(np.float64)).astype(np.float32).astype(BF)
    return np.stack([high, low])


@functools.lru_cache(maxsize=1)
def make_tables():
    outer = np.arange(ROWS)[:, None] * np.arange(HALF)[None, :] % OUTER
    angle = -2.0 * np.pi / OUTER * outer
    eye = np.eye(CH)
    first = np.concatenate([np.kron(np.cos(angle), eye), np.kron(np.sin(angle), eye)], axis=0)
    inner = np.arange(LANE)[:, None] * np.arange(LANE)[None, :] % LANE
    inner_cos = np.cos(2.0 * np.pi / LANE * inner)
    inner_sin = np.sin(-2.0 * np.pi / LANE * inner)
    second = np.block([[inner_cos, inner_sin], [-inner_sin, inner_cos]])
    turn = -2.0 * np.pi / PADDED * (np.arange(ROWS)[:, None] * np.arange(LANE)[None, :])
    turn = np.repeat(turn, CH, axis=0)
    twist = np.stack([np.cos(turn), np.sin(turn)]).astype(np.float32)
    count = np.full((ROWS,), 2.0)
    count[0] = count[-1] = 1.0
    back = count[None, :] / PADDED
    last = np.concatenate(
        [np.kron(np.cos(angle).T * back, eye), np.kron(np.sin(angle).T * back, eye)], axis=1
    )
    return (halves(first), halves(second), halves(second.T), twist, halves(last))


def split(x):
    high = x.astype(BF)
    return high, (x - high.astype(F32)).astype(BF)


def dot(a, b):
    return jnp.dot(a, b, preferred_element_type=F32)


def dot3(a, table):
    high, low = split(a)
    return dot(high, table[0]) + (dot(low, table[0]) + dot(high, table[1]))


def table_dot3(table, b):
    high, low = split(b)
    return dot(table[0], high) + (dot(table[0], low) + dot(table[1], high))


N = ROWS * CH


def spread(mid, twist, col):
    real = mid[:N, col : col + LANE]
    imag = mid[N:, col : col + LANE]
    return jnp.concatenate(
        [real * twist[0] - imag * twist[1], real * twist[1] + imag * twist[0]], axis=1
    )


def unspread(mid, twist):
    real = mid[:, :LANE]
    imag = mid[:, LANE:]
    return jnp.concatenate(
        [real * twist[0] + imag * twist[1], imag * twist[0] - real * twist[1]], axis=0
    )


def times(a, b):
    ar, ai, br, bi = a[:, :LANE], a[:, LANE:], b[:, :LANE], b[:, LANE:]
    return jnp.concatenate([ar * br - ai * bi, ar * bi + ai * br], axis=1)


def times_conj(a, b):
    ar, ai, br, bi = a[:, :LANE], a[:, LANE:], b[:, :LANE], b[:, LANE:]
    return jnp.concatenate([ar * br + ai * bi, ai * br - ar * bi], axis=1)


def pack_kernel(key, value, weight, out):
    product = key[...].astype(F32) * value[...].astype(F32)
    for i, signal in enumerate((product, weight[...] * (1.0 / math.sqrt(LENGTH)))):
        out[:, i * CH : (i + 1) * CH, :] = signal.T.astype(BF).reshape(HALF, CH, LANE)


def turn_kernel(query, out):
    out[...] = query[...].astype(F32).T.astype(BF)


def share_kernel(cot, out):
    k = lax.axis_index("k")
    for h in range(H):
        for j in range(K):
            side = pl.multiple_of((2 * h + (k + j) % 2) * LANE, LANE)
            piece = cot[:, pl.ds(side, LANE)]
            for c in range(C):
                out[h * C + c, :, j * LANE : (j + 1) * LANE] = piece


def conv_kernel(packed, first, second, second_back, twist, last, conv, spectra):
    product = packed[:, 0:CH, :].reshape(HALF * CH, LANE)
    weight = packed[:, CH:, :].reshape(HALF * CH, LANE)
    both = jnp.concatenate([product, weight], axis=1)
    mid = dot(first[0], both) + dot(first[1], both)
    spec = dot3(
        jnp.concatenate([spread(mid, twist, 0), spread(mid, twist, LANE)], axis=0), second
    )
    spectra[...] = spec
    turned = unspread(dot3(times(spec[:N], spec[N:]), second_back), twist)
    conv[...] = table_dot3(last, turned).astype(BF)


def partial_grad(weights, cot, side):
    total = jnp.zeros((WIDE, H * LANE), F32)
    columns = slice(side * LANE, (side + 1) * LANE)
    for z in range(0, Z, 2):
        weight = jnp.concatenate([weights[z], weights[z + 1]], axis=1)
        rows = [
            jnp.concatenate([cot[h * C + z, :, columns], cot[h * C + z + 1, :, columns]], axis=1)
            for h in range(H)
        ]
        total = total + lax.dot_general(
            weight,
            jnp.concatenate(rows, axis=0),
            (((1,), (1,)), ((), ())),
            preferred_element_type=F32,
        )
    return total


def own_grad_kernel(own, cot, out):
    out[...] = partial_grad(own, cot, 0)


def grad_kernel(first, other, cot, conv, query, query_pair, out, kept, sent):
    here = lax.axis_index("h")
    for z in range(Z):
        for h in range(H):
            for k in range(K):
                for part in range(2):
                    a = 4 * z + 2 * part + k
                    out[4 * z + 2 * h + k, part * CH : (part + 1) * CH, :] = conv[
                        a * CH : (a + 1) * CH, :
                    ]
    total = (first[...] + partial_grad(other, cot, 1)) * SCALE
    left, right = total[:, :LANE], total[:, LANE:]
    kept[...] = jnp.where(here == 0, left, right)
    sent[...] = jnp.where(here == 0, right, left).astype(BF)
    for part, side in enumerate((left, right)):
        gate = jnp.where(here == part, query[...].astype(F32), query_pair[...].astype(F32))
        grad = (side * gate).astype(BF)
        out[:, (2 + part) * CH : (3 + part) * CH, :] = grad.reshape(HALF, CH, LANE)


def tile_of(moved, query, query_pair):
    here = lax.axis_index("h")
    parts = []
    for p in range(2):
        conv = moved[:, p * CH : (p + 1) * CH, :].reshape(WIDE, LANE).astype(F32)
        gate = jnp.where(here == p, query[...].astype(F32), query_pair[...].astype(F32))
        parts.append((gate * conv).astype(BF))
    return jnp.concatenate(parts, axis=1)


def project_kernel(moved, query, query_pair, own, other, out):
    mixed = tile_of(moved, query, query_pair).astype(F32).T.astype(BF)
    for z in range(Z):
        weight = jnp.concatenate([own[z], other[z]], axis=1)
        part = (dot(mixed, weight) * SCALE).astype(BF)
        for h in range(H):
            out[h * C + z] = part[h * LANE : (h + 1) * LANE]


def weight_kernel(moved, moved_other, query, pair, query_other, pair_other, cot, cot_other, out):
    mixed = jnp.concatenate(
        [tile_of(moved, query, pair), tile_of(moved_other, query_other, pair_other)], axis=1
    )
    for z in range(0, Z, 2):
        columns = []
        for y in (z, z + 1):
            rows = [cot[h * C + y, :, :LANE] for h in range(H)]
            rows += [cot_other[h * C + y, :, LANE:] for h in range(H)]
            columns.append(jnp.concatenate(rows, axis=0))
        grad = dot(mixed, jnp.concatenate(columns, axis=1)) * SCALE
        out[z] = grad[:, :LANE].astype(out.dtype)
        out[z + 1] = grad[:, LANE:].astype(out.dtype)


def back_kernel(moved, spectra, first, second, second_back, twist, last, out):
    pieces = []
    for z in range(Z):
        for part in range(2):
            for k in range(K):
                low = (2 + part) * CH
                pieces.append(
                    moved[4 * z + k, low : low + CH, :].astype(F32)
                    + moved[4 * z + 2 + k, low : low + CH, :].astype(F32)
                )
    high, low = split(jnp.concatenate(pieces, axis=0))
    sides = dot(first[0], jnp.concatenate([high, low], axis=1))
    mid = sides[:, :LANE] + (sides[:, LANE:] + dot(first[1], high))
    grad = dot3(spread(mid, twist, 0), second)
    product_spec, filter_spec = spectra[:N], spectra[N:]
    both = dot3(
        jnp.concatenate([times_conj(grad, filter_spec), times_conj(grad, product_spec)], axis=0),
        second_back,
    )
    turned = jnp.concatenate([unspread(both[:N], twist), unspread(both[N:], twist)], axis=1)
    result = table_dot3(last, turned).astype(BF)
    out[:, 0:CH, :] = result[:, :LANE].reshape(HALF, CH, LANE)
    out[:, CH:, :] = result[:, LANE:].reshape(HALF, CH, LANE)


def finish_kernel(moved, key, value, key_grad, value_grad, filter_grad):
    def turned(i):
        return moved[:, i * CH : (i + 1) * CH, :].reshape(WIDE, LANE).astype(F32).T

    product_grad = turned(0)
    key_grad[...] = (product_grad * value[...].astype(F32)).astype(BF)
    value_grad[...] = (product_grad * key[...].astype(F32)).astype(BF)
    filter_grad[...] = turned(1) * (1.0 / math.sqrt(LENGTH))


def sum_kernel(parts, moved, kept, received, out, query_grad):
    k = lax.axis_index("k")
    for h in range(H):
        total = parts[h * C].astype(F32)
        for c in range(1, C):
            total = total + parts[h * C + c].astype(F32)
        total = total.astype(BF)
        for j in range(K):
            side = pl.multiple_of((2 * h + (k + j) % 2) * LANE, LANE)
            out[:, pl.ds(side, LANE)] = total[:, j * LANE : (j + 1) * LANE]
    left = moved[:, 0:CH, :].reshape(WIDE, LANE).astype(F32)
    right = moved[:, CH : 2 * CH, :].reshape(WIDE, LANE).astype(F32)
    conv = jnp.where(lax.axis_index("h") == 0, left, right)
    grad = (kept[...] + received[...].astype(F32)) * conv
    query_grad[...] = grad.T.astype(BF)


class Late:
    def __init__(self, ref, buffer, semaphore):
        self.buffer, self.copy, self.waiting = buffer, pltpu.make_async_copy(ref, buffer, semaphore), True
        self.copy.start()

    def __getitem__(self, index):
        if self.waiting:
            self.copy.wait()
            self.waiting = False
        return self.buffer[index]


class Stream:
    def __init__(self, ref, buffer, semaphores):
        self.ref, self.buffer, self.semaphores, self.copies = ref, buffer, semaphores, []
        self.dtype = ref.dtype

    def __setitem__(self, index, value):
        self.buffer[index] = value
        copy = pltpu.make_async_copy(
            self.buffer.at[index], self.ref.at[index], self.semaphores.at[len(self.copies)]
        )
        copy.start()
        self.copies.append(copy)


def call(kernel, outs, *args, flops=0, late=(), grant=GRANT, stream=False):
    shapes = tuple(jax.ShapeDtypeStruct(s, d) for s, d in outs)
    count = len(args) + len(outs)

    def body(*refs):
        refs, rest = list(refs[:count]), list(refs[count:])
        for i, at in enumerate(late):
            refs[at] = Late(refs[at], rest[i], rest[len(late)].at[i])
        if stream:
            refs[-1] = Stream(refs[-1], rest[-2], rest[-1])
        kernel(*refs)
        for at in late:
            if refs[at].waiting:
                refs[at].copy.wait()
        if stream:
            for copy in refs[-1].copies:
                copy.wait()

    scratch = [pltpu.VMEM(args[at].shape, args[at].dtype) for at in late]
    if late:
        scratch.append(pltpu.SemaphoreType.DMA((len(late),)))
    if stream:
        scratch += [pltpu.VMEM(*outs[0]), pltpu.SemaphoreType.DMA((outs[0][0][0],))]
    out_space = pltpu.HBM if stream else pltpu.VMEM
    return pl.pallas_call(
        body,
        out_shape=shapes,
        in_specs=[
            pl.BlockSpec(memory_space=pltpu.HBM if i in late else pltpu.VMEM)
            for i in range(len(args))
        ],
        out_specs=tuple([pl.BlockSpec(memory_space=out_space)] * len(outs)),
        scratch_shapes=scratch,
        compiler_params=pltpu.CompilerParams(vmem_limit_bytes=grant),
        cost_estimate=pl.CostEstimate(flops=flops, bytes_accessed=4 << 20, transcendentals=0),
        name=kernel.__name__,
    )(*args)


def exchange(x, axes):
    return lax.all_to_all(x, axes, split_axis=0, concat_axis=0, tiled=True)


def local(queries, keys, values, filter_weight, out_weight, cotangent):
    first, second, second_back, twist, last = make_tables()
    core_pair = [(0, 1), (1, 0)]
    (packed,) = call(
        pack_kernel, [((HALF, 2 * CH, LANE), BF)], keys, values, filter_weight,
        late=(0, 1, 2), grant=FULL,
    )
    (query_t,) = call(turn_kernel, [((WIDE, LANE), BF)], queries)
    (shared,) = call(share_kernel, [((H * C, LANE, K * LANE), BF)], cotangent)
    query = (query_t, lax.ppermute(query_t, "h", core_pair))
    own = lax.all_gather(out_weight, "z")
    packed = exchange(packed, SEQ)
    packed, shared, query = lax.optimization_barrier((packed, shared, query))
    query_other = tuple(lax.ppermute(side, "k", core_pair) for side in query)
    cot = exchange(shared, PLANE)
    conv, spectra = call(
        conv_kernel,
        [((HALF * CH, LANE), BF), ((2 * N, 2 * LANE), F32)],
        packed, first, second, second_back, twist, last, flops=5_000_000_000, late=(1, 2, 3, 4, 5),
    )
    own, cot, conv = lax.optimization_barrier((own, cot, conv))
    other = lax.ppermute(own, "k", core_pair)
    cot_other = lax.ppermute(cot, "k", core_pair)
    (own_part,) = call(own_grad_kernel, [((WIDE, H * LANE), F32)], own, cot)
    sent, kept, passed = call(
        grad_kernel,
        [((HALF, 4 * CH, LANE), BF), ((WIDE, LANE), F32), ((WIDE, LANE), BF)],
        own_part, other, cot, conv, *query,
    )
    received = lax.ppermute(passed, "h", core_pair)
    moved = exchange(sent, SEQ)
    moved_other = lax.ppermute(moved, "k", core_pair)
    (out_part,) = call(project_kernel, [((H * C, LANE, K * LANE), BF)], moved, *query, own, other)
    moved_other, _ = lax.optimization_barrier((moved_other, out_part))
    (weight_part,) = call(
        weight_kernel,
        [((Z, WIDE, LANE), F32)],
        moved, moved_other, *query, *query_other, cot, cot_other, stream=True,
    )
    weight_grad = lax.psum_scatter(
        weight_part.reshape(Z * WIDE, LANE), "z", scatter_dimension=0, tiled=True
    )
    out_parts = exchange(out_part, PLANE)
    (back,) = call(
        back_kernel, [((HALF, 2 * CH, LANE), BF)],
        moved, spectra, first, second, second_back, twist, last, flops=8_000_000_000,
        late=(1, 2, 3, 4, 5, 6),
    )
    back, out_parts = lax.optimization_barrier((back, out_parts))
    back = exchange(back, SEQ)
    block_out, query_grad = call(
        sum_kernel,
        [((LANE, WIDE), BF), ((LANE, WIDE), BF)],
        out_parts, moved, kept, received,
    )
    key_grad, value_grad, filter_grad = call(
        finish_kernel,
        [((LANE, WIDE), BF), ((LANE, WIDE), BF), ((LANE, WIDE), F32)],
        back, keys, values,
    )
    return (block_out, query_grad, key_grad, value_grad, filter_grad, weight_grad)


def solution(mesh):
    split_mesh = Mesh(mesh.devices.reshape(Z, H, K, C), ("z", "h", "k", "chan"))
    by_position = P(SEQ, "chan")
    by_channel = P("chan", SEQ)
    in_specs = (by_position,) * 4 + (by_channel, by_position)
    out_specs = (by_position,) * 5 + (by_channel,)
    return jax.shard_map(
        local, mesh=split_mesh, in_specs=in_specs, out_specs=out_specs, check_vma=False
    )
```

```python
import functools
import math

import jax
import jax.numpy as jnp
import numpy as np
from jax import lax
from jax.experimental import pallas as pl
from jax.experimental.pallas import tpu as pltpu
from jax.sharding import Mesh
from jax.sharding import PartitionSpec as P

D = 4096
LENGTH = 4096
PADDED = 2 * LENGTH
LANE = 128
OUTER = PADDED // LANE
HALF = OUTER // 2
ROWS = HALF + 1
CH = 16
WIDE = 512
Z, H, K, C = 8, 2, 2, 8
SEQ = ("z", "h", "k")
PLANE = ("h", "chan")
BF = jnp.bfloat16
F32 = jnp.float32
SCALE = 1.0 / math.sqrt(D)
GRANT = 40 * 1024 * 1024
FULL = 64 * 1024 * 1024


def halves(table):
    high = np.asarray(table, np.float32).astype(BF)
    low = (np.asarray(table, np.float64) - high.astype(np.float64)).astype(np.float32).astype(BF)
    return np.stack([high, low])


@functools.lru_cache(maxsize=1)
def make_tables():
    outer = np.arange(ROWS)[:, None] * np.arange(HALF)[None, :] % OUTER
    angle = -2.0 * np.pi / OUTER * outer
    eye = np.eye(CH)
    first = np.concatenate([np.kron(np.cos(angle), eye), np.kron(np.sin(angle), eye)], axis=0)
    inner = np.arange(LANE)[:, None] * np.arange(LANE)[None, :] % LANE
    inner_cos = np.cos(2.0 * np.pi / LANE * inner)
    inner_sin = np.sin(-2.0 * np.pi / LANE * inner)
    second = np.block([[inner_cos, inner_sin], [-inner_sin, inner_cos]])
    turn = -2.0 * np.pi / PADDED * (np.arange(ROWS)[:, None] * np.arange(LANE)[None, :])
    turn = np.repeat(turn, CH, axis=0)
    twist = np.stack([np.cos(turn), np.sin(turn)]).astype(np.float32)
    count = np.full((ROWS,), 2.0)
    count[0] = count[-1] = 1.0
    back = count[None, :] / PADDED
    last = np.concatenate(
        [np.kron(np.cos(angle).T * back, eye), np.kron(np.sin(angle).T * back, eye)], axis=1
    )
    return (halves(first), halves(second), halves(second.T), twist, halves(last))


def split(x):
    high = x.astype(BF)
    return high, (x - high.astype(F32)).astype(BF)


def dot(a, b):
    return jnp.dot(a, b, preferred_element_type=F32)


def dot3(a, table):
    high, low = split(a)
    return dot(high, table[0]) + (dot(low, table[0]) + dot(high, table[1]))


def table_dot3(table, b):
    high, low = split(b)
    return dot(table[0], high) + (dot(table[0], low) + dot(table[1], high))


N = ROWS * CH


def spread(mid, twist, col):
    real = mid[:N, col : col + LANE]
    imag = mid[N:, col : col + LANE]
    return jnp.concatenate(
        [real * twist[0] - imag * twist[1], real * twist[1] + imag * twist[0]], axis=1
    )


def unspread(mid, twist):
    real = mid[:, :LANE]
    imag = mid[:, LANE:]
    return jnp.concatenate(
        [real * twist[0] + imag * twist[1], imag * twist[0] - real * twist[1]], axis=0
    )


def times(a, b):
    ar, ai, br, bi = a[:, :LANE], a[:, LANE:], b[:, :LANE], b[:, LANE:]
    return jnp.concatenate([ar * br - ai * bi, ar * bi + ai * br], axis=1)


def times_conj(a, b):
    ar, ai, br, bi = a[:, :LANE], a[:, LANE:], b[:, :LANE], b[:, LANE:]
    return jnp.concatenate([ar * br + ai * bi, ai * br - ar * bi], axis=1)


def pack_kernel(key, value, weight, out):
    product = key[...].astype(F32) * value[...].astype(F32)
    for i, signal in enumerate((product, weight[...] * (1.0 / math.sqrt(LENGTH)))):
        out[:, i * CH : (i + 1) * CH, :] = signal.T.astype(BF).reshape(HALF, CH, LANE)


def turn_kernel(query, out):
    out[...] = query[...].astype(F32).T.astype(BF)


def share_kernel(cot, out):
    k = lax.axis_index("k")
    for h in range(H):
        for j in range(K):
            side = pl.multiple_of((2 * h + (k + j) % 2) * LANE, LANE)
            piece = cot[:, pl.ds(side, LANE)]
            for c in range(C):
                out[h * C + c, :, j * LANE : (j + 1) * LANE] = piece


def conv_kernel(packed, first, second, second_back, twist, last, conv, spectra):
    product = packed[:, 0:CH, :].reshape(HALF * CH, LANE)
    weight = packed[:, CH:, :].reshape(HALF * CH, LANE)
    both = jnp.concatenate([product, weight], axis=1)
    mid = dot(first[0], both) + dot(first[1], both)
    spec = dot3(
        jnp.concatenate([spread(mid, twist, 0), spread(mid, twist, LANE)], axis=0), second
    )
    spectra[...] = spec
    turned = unspread(dot3(times(spec[:N], spec[N:]), second_back), twist)
    conv[...] = table_dot3(last, turned).astype(BF)


def partial_grad(weights, cot, side):
    total = jnp.zeros((WIDE, H * LANE), F32)
    columns = slice(side * LANE, (side + 1) * LANE)
    for z in range(0, Z, 2):
        weight = jnp.concatenate([weights[z], weights[z + 1]], axis=1)
        rows = [
            jnp.concatenate([cot[h * C + z, :, columns], cot[h * C + z + 1, :, columns]], axis=1)
            for h in range(H)
        ]
        total = total + lax.dot_general(
            weight,
            jnp.concatenate(rows, axis=0),
            (((1,), (1,)), ((), ())),
            preferred_element_type=F32,
        )
    return total


def own_grad_kernel(own, cot, out, side):
    side[...] = cot[:, :, LANE:]
    out[...] = partial_grad(own, cot, 0)


def grad_kernel(first, other, cot, conv, query, query_pair, out, kept, sent):
    here = lax.axis_index("h")
    for z in range(Z):
        for h in range(H):
            for k in range(K):
                for part in range(2):
                    a = 4 * z + 2 * part + k
                    out[4 * z + 2 * h + k, part * CH : (part + 1) * CH, :] = conv[
                        a * CH : (a + 1) * CH, :
                    ]
    total = (first[...] + partial_grad(other, cot, 1)) * SCALE
    left, right = total[:, :LANE], total[:, LANE:]
    kept[...] = jnp.where(here == 0, left, right)
    sent[...] = jnp.where(here == 0, right, left).astype(BF)
    for part, side in enumerate((left, right)):
        gate = jnp.where(here == part, query[...].astype(F32), query_pair[...].astype(F32))
        grad = (side * gate).astype(BF)
        out[:, (2 + part) * CH : (3 + part) * CH, :] = grad.reshape(HALF, CH, LANE)


def tile_of(moved, query, query_pair):
    here = lax.axis_index("h")
    parts = []
    for p in range(2):
        conv = moved[:, p * CH : (p + 1) * CH, :].reshape(WIDE, LANE).astype(F32)
        gate = jnp.where(here == p, query[...].astype(F32), query_pair[...].astype(F32))
        parts.append((gate * conv).astype(BF))
    return jnp.concatenate(parts, axis=1)


def project_kernel(moved, query, query_pair, own, other, out):
    mixed = tile_of(moved, query, query_pair).astype(F32).T.astype(BF)
    for z in range(Z):
        weight = jnp.concatenate([own[z], other[z]], axis=1)
        part = (dot(mixed, weight) * SCALE).astype(BF)
        for h in range(H):
            out[h * C + z] = part[h * LANE : (h + 1) * LANE]


def weight_kernel(moved, moved_other, query, pair, query_other, pair_other, cot, cot_other, out):
    mixed = jnp.concatenate(
        [tile_of(moved, query, pair), tile_of(moved_other, query_other, pair_other)], axis=1
    )
    for z in range(0, Z, 2):
        columns = []
        for y in (z, z + 1):
            rows = [cot[h * C + y, :, :LANE] for h in range(H)]
            rows += [cot_other[h * C + y] for h in range(H)]
            columns.append(jnp.concatenate(rows, axis=0))
        grad = dot(mixed, jnp.concatenate(columns, axis=1)) * SCALE
        out[z] = grad[:, :LANE].astype(out.dtype)
        out[z + 1] = grad[:, LANE:].astype(out.dtype)


def back_kernel(moved, spectra, first, second, second_back, twist, last, out):
    pieces = []
    for z in range(Z):
        for part in range(2):
            for k in range(K):
                low = (2 + part) * CH
                pieces.append(
                    moved[4 * z + k, low : low + CH, :].astype(F32)
                    + moved[4 * z + 2 + k, low : low + CH, :].astype(F32)
                )
    high, low = split(jnp.concatenate(pieces, axis=0))
    sides = dot(first[0], jnp.concatenate([high, low], axis=1))
    mid = sides[:, :LANE] + (sides[:, LANE:] + dot(first[1], high))
    grad = dot3(spread(mid, twist, 0), second)
    product_spec, filter_spec = spectra[:N], spectra[N:]
    both = dot3(
        jnp.concatenate([times_conj(grad, filter_spec), times_conj(grad, product_spec)], axis=0),
        second_back,
    )
    turned = jnp.concatenate([unspread(both[:N], twist), unspread(both[N:], twist)], axis=1)
    result = table_dot3(last, turned).astype(BF)
    out[:, 0:CH, :] = result[:, :LANE].reshape(HALF, CH, LANE)
    out[:, CH:, :] = result[:, LANE:].reshape(HALF, CH, LANE)


def finish_kernel(moved, key, value, key_grad, value_grad, filter_grad):
    def turned(i):
        return moved[:, i * CH : (i + 1) * CH, :].reshape(WIDE, LANE).astype(F32).T

    product_grad = turned(0)
    key_grad[...] = (product_grad * value[...].astype(F32)).astype(BF)
    value_grad[...] = (product_grad * key[...].astype(F32)).astype(BF)
    filter_grad[...] = turned(1) * (1.0 / math.sqrt(LENGTH))


def sum_kernel(parts, moved, kept, received, out, query_grad):
    k = lax.axis_index("k")
    for h in range(H):
        total = parts[h * C].astype(F32)
        for c in range(1, C):
            total = total + parts[h * C + c].astype(F32)
        total = total.astype(BF)
        for j in range(K):
            side = pl.multiple_of((2 * h + (k + j) % 2) * LANE, LANE)
            out[:, pl.ds(side, LANE)] = total[:, j * LANE : (j + 1) * LANE]
    left = moved[:, 0:CH, :].reshape(WIDE, LANE).astype(F32)
    right = moved[:, CH : 2 * CH, :].reshape(WIDE, LANE).astype(F32)
    conv = jnp.where(lax.axis_index("h") == 0, left, right)
    grad = (kept[...] + received[...].astype(F32)) * conv
    query_grad[...] = grad.T.astype(BF)


class Late:
    def __init__(self, ref, buffer, semaphore):
        self.buffer, self.copy, self.waiting = buffer, pltpu.make_async_copy(ref, buffer, semaphore), True
        self.copy.start()

    def __getitem__(self, index):
        if self.waiting:
            self.copy.wait()
            self.waiting = False
        return self.buffer[index]


class Stream:
    def __init__(self, ref, buffer, semaphores):
        self.ref, self.buffer, self.semaphores, self.copies = ref, buffer, semaphores, []
        self.dtype = ref.dtype

    def __setitem__(self, index, value):
        self.buffer[index] = value
        copy = pltpu.make_async_copy(
            self.buffer.at[index], self.ref.at[index], self.semaphores.at[len(self.copies)]
        )
        copy.start()
        self.copies.append(copy)


def call(kernel, outs, *args, flops=0, late=(), grant=GRANT, stream=False):
    shapes = tuple(jax.ShapeDtypeStruct(s, d) for s, d in outs)
    count = len(args) + len(outs)

    def body(*refs):
        refs, rest = list(refs[:count]), list(refs[count:])
        for i, at in enumerate(late):
            refs[at] = Late(refs[at], rest[i], rest[len(late)].at[i])
        if stream:
            refs[-1] = Stream(refs[-1], rest[-2], rest[-1])
        kernel(*refs)
        for at in late:
            if refs[at].waiting:
                refs[at].copy.wait()
        if stream:
            for copy in refs[-1].copies:
                copy.wait()

    scratch = [pltpu.VMEM(args[at].shape, args[at].dtype) for at in late]
    if late:
        scratch.append(pltpu.SemaphoreType.DMA((len(late),)))
    if stream:
        scratch += [pltpu.VMEM(*outs[0]), pltpu.SemaphoreType.DMA((outs[0][0][0],))]
    out_space = pltpu.HBM if stream else pltpu.VMEM
    return pl.pallas_call(
        body,
        out_shape=shapes,
        in_specs=[
            pl.BlockSpec(memory_space=pltpu.HBM if i in late else pltpu.VMEM)
            for i in range(len(args))
        ],
        out_specs=tuple([pl.BlockSpec(memory_space=out_space)] * len(outs)),
        scratch_shapes=scratch,
        compiler_params=pltpu.CompilerParams(vmem_limit_bytes=grant),
        cost_estimate=pl.CostEstimate(flops=flops, bytes_accessed=4 << 20, transcendentals=0),
        name=kernel.__name__,
    )(*args)


def exchange(x, axes):
    return lax.all_to_all(x, axes, split_axis=0, concat_axis=0, tiled=True)


def local(queries, keys, values, filter_weight, out_weight, cotangent):
    first, second, second_back, twist, last = make_tables()
    core_pair = [(0, 1), (1, 0)]
    (packed,) = call(
        pack_kernel, [((HALF, 2 * CH, LANE), BF)], keys, values, filter_weight,
        late=(0, 1, 2), grant=FULL,
    )
    (query_t,) = call(turn_kernel, [((WIDE, LANE), BF)], queries)
    (shared,) = call(share_kernel, [((H * C, LANE, K * LANE), BF)], cotangent)
    query = (query_t, lax.ppermute(query_t, "h", core_pair))
    own = lax.all_gather(out_weight, "z")
    packed = exchange(packed, SEQ)
    packed, shared, query = lax.optimization_barrier((packed, shared, query))
    query_other = tuple(lax.ppermute(side, "k", core_pair) for side in query)
    cot = exchange(shared, PLANE)
    conv, spectra = call(
        conv_kernel,
        [((HALF * CH, LANE), BF), ((2 * N, 2 * LANE), F32)],
        packed, first, second, second_back, twist, last, flops=5_000_000_000, late=(1, 2, 3, 4, 5),
    )
    own, cot, conv = lax.optimization_barrier((own, cot, conv))
    other = lax.ppermute(own, "k", core_pair)
    own_part, side = call(
        own_grad_kernel,
        [((WIDE, H * LANE), F32), ((H * C, LANE, LANE), BF)],
        own, cot,
    )
    sent, kept, passed = call(
        grad_kernel,
        [((HALF, 4 * CH, LANE), BF), ((WIDE, LANE), F32), ((WIDE, LANE), BF)],
        own_part, other, cot, conv, *query,
    )
    cot_other = lax.ppermute(side, "k", core_pair)
    received = lax.ppermute(passed, "h", core_pair)
    moved = exchange(sent, SEQ)
    moved_other = lax.ppermute(moved, "k", core_pair)
    (out_part,) = call(project_kernel, [((H * C, LANE, K * LANE), BF)], moved, *query, own, other)
    moved_other, _ = lax.optimization_barrier((moved_other, out_part))
    (weight_part,) = call(
        weight_kernel,
        [((Z, WIDE, LANE), F32)],
        moved, moved_other, *query, *query_other, cot, cot_other, late=(7,), stream=True,
    )
    weight_grad = lax.psum_scatter(
        weight_part.reshape(Z * WIDE, LANE), "z", scatter_dimension=0, tiled=True
    )
    out_parts = exchange(out_part, PLANE)
    (back,) = call(
        back_kernel, [((HALF, 2 * CH, LANE), BF)],
        moved, spectra, first, second, second_back, twist, last, flops=8_000_000_000,
        late=(1, 2, 3, 4, 5, 6),
    )
    back, out_parts = lax.optimization_barrier((back, out_parts))
    back = exchange(back, SEQ)
    block_out, query_grad = call(
        sum_kernel,
        [((LANE, WIDE), BF), ((LANE, WIDE), BF)],
        out_parts, moved, kept, received,
    )
    key_grad, value_grad, filter_grad = call(
        finish_kernel,
        [((LANE, WIDE), BF), ((LANE, WIDE), BF), ((LANE, WIDE), F32)],
        back, keys, values,
    )
    return (block_out, query_grad, key_grad, value_grad, filter_grad, weight_grad)


def solution(mesh):
    split_mesh = Mesh(mesh.devices.reshape(Z, H, K, C), ("z", "h", "k", "chan"))
    by_position = P(SEQ, "chan")
    by_channel = P("chan", SEQ)
    in_specs = (by_position,) * 4 + (by_channel, by_position)
    out_specs = (by_position,) * 5 + (by_channel,)
    return jax.shard_map(
        local, mesh=split_mesh, in_specs=in_specs, out_specs=out_specs, check_vma=False
    )
```

```python
import functools
import math

import jax
import jax.numpy as jnp
import numpy as np
from jax import lax
from jax.experimental import pallas as pl
from jax.experimental.pallas import tpu as pltpu
from jax.sharding import Mesh
from jax.sharding import PartitionSpec as P

D = 4096
LENGTH = 4096
PADDED = 2 * LENGTH
LANE = 128
OUTER = PADDED // LANE
HALF = OUTER // 2
ROWS = HALF + 1
CH = 16
WIDE = 512
Z, H, K, C = 8, 2, 2, 8
SEQ = ("z", "h", "k")
PLANE = ("h", "chan")
BF = jnp.bfloat16
F32 = jnp.float32
SCALE = 1.0 / math.sqrt(D)
GRANT = 40 * 1024 * 1024
FULL = 64 * 1024 * 1024


def halves(table):
    high = np.asarray(table, np.float32).astype(BF)
    low = (np.asarray(table, np.float64) - high.astype(np.float64)).astype(np.float32).astype(BF)
    return np.stack([high, low])


@functools.lru_cache(maxsize=1)
def make_tables():
    outer = np.arange(ROWS)[:, None] * np.arange(HALF)[None, :] % OUTER
    angle = -2.0 * np.pi / OUTER * outer
    eye = np.eye(CH)
    first = np.concatenate([np.kron(np.cos(angle), eye), np.kron(np.sin(angle), eye)], axis=0)
    inner = np.arange(LANE)[:, None] * np.arange(LANE)[None, :] % LANE
    inner_cos = np.cos(2.0 * np.pi / LANE * inner)
    inner_sin = np.sin(-2.0 * np.pi / LANE * inner)
    second = np.block([[inner_cos, inner_sin], [-inner_sin, inner_cos]])
    turn = -2.0 * np.pi / PADDED * (np.arange(ROWS)[:, None] * np.arange(LANE)[None, :])
    turn = np.repeat(turn, CH, axis=0)
    twist = np.stack([np.cos(turn), np.sin(turn)]).astype(np.float32)
    count = np.full((ROWS,), 2.0)
    count[0] = count[-1] = 1.0
    back = count[None, :] / PADDED
    last = np.concatenate(
        [np.kron(np.cos(angle).T * back, eye), np.kron(np.sin(angle).T * back, eye)], axis=1
    )
    return (halves(first), halves(second), halves(second.T), twist, halves(last))


def split(x):
    high = x.astype(BF)
    return high, (x - high.astype(F32)).astype(BF)


def dot(a, b):
    return jnp.dot(a, b, preferred_element_type=F32)


def dot3(a, table):
    high, low = split(a)
    return dot(high, table[0]) + (dot(low, table[0]) + dot(high, table[1]))


def table_dot3(table, b):
    high, low = split(b)
    return dot(table[0], high) + (dot(table[0], low) + dot(table[1], high))


N = ROWS * CH


def spread(mid, twist, col):
    real = mid[:N, col : col + LANE]
    imag = mid[N:, col : col + LANE]
    return jnp.concatenate(
        [real * twist[0] - imag * twist[1], real * twist[1] + imag * twist[0]], axis=1
    )


def unspread(mid, twist):
    real = mid[:, :LANE]
    imag = mid[:, LANE:]
    return jnp.concatenate(
        [real * twist[0] + imag * twist[1], imag * twist[0] - real * twist[1]], axis=0
    )


def times(a, b):
    ar, ai, br, bi = a[:, :LANE], a[:, LANE:], b[:, :LANE], b[:, LANE:]
    return jnp.concatenate([ar * br - ai * bi, ar * bi + ai * br], axis=1)


def times_conj(a, b):
    ar, ai, br, bi = a[:, :LANE], a[:, LANE:], b[:, :LANE], b[:, LANE:]
    return jnp.concatenate([ar * br + ai * bi, ai * br - ar * bi], axis=1)


def pack_kernel(key, value, weight, out):
    product = key[...].astype(F32) * value[...].astype(F32)
    for i, signal in enumerate((product, weight[...] * (1.0 / math.sqrt(LENGTH)))):
        out[:, i * CH : (i + 1) * CH, :] = signal.T.astype(BF).reshape(HALF, CH, LANE)


def turn_kernel(query, out):
    out[...] = query[...].astype(F32).T.astype(BF)


def share_kernel(cot, out):
    k = lax.axis_index("k")
    for h in range(H):
        for j in range(K):
            side = pl.multiple_of((2 * h + (k + j) % 2) * LANE, LANE)
            piece = cot[:, pl.ds(side, LANE)]
            for c in range(C):
                out[h * C + c, :, j * LANE : (j + 1) * LANE] = piece


def conv_kernel(packed, first, second, second_back, twist, last, conv, spectra):
    product = packed[:, 0:CH, :].reshape(HALF * CH, LANE)
    weight = packed[:, CH:, :].reshape(HALF * CH, LANE)
    both = jnp.concatenate([product, weight], axis=1)
    mid = dot(first[0], both) + dot(first[1], both)
    spec = dot3(
        jnp.concatenate([spread(mid, twist, 0), spread(mid, twist, LANE)], axis=0), second
    )
    spectra[...] = spec
    turned = unspread(dot3(times(spec[:N], spec[N:]), second_back), twist)
    conv[...] = table_dot3(last, turned).astype(BF)


def partial_grad(weights, cot, side):
    total = jnp.zeros((WIDE, H * LANE), F32)
    columns = slice(side * LANE, (side + 1) * LANE)
    for z in range(0, Z, 2):
        weight = jnp.concatenate([weights[z], weights[z + 1]], axis=1)
        rows = [
            jnp.concatenate([cot[h * C + z, :, columns], cot[h * C + z + 1, :, columns]], axis=1)
            for h in range(H)
        ]
        total = total + lax.dot_general(
            weight,
            jnp.concatenate(rows, axis=0),
            (((1,), (1,)), ((), ())),
            preferred_element_type=F32,
        )
    return total


def own_grad_kernel(own, cot, out, side):
    side[...] = cot[:, :, LANE:]
    out[...] = partial_grad(own, cot, 0)


def grad_kernel(first, other, cot, conv, query, query_pair, out, kept, sent):
    here = lax.axis_index("h")
    for z in range(Z):
        for h in range(H):
            for k in range(K):
                for part in range(2):
                    a = 4 * z + 2 * part + k
                    out[4 * z + 2 * h + k, part * CH : (part + 1) * CH, :] = conv[
                        a * CH : (a + 1) * CH, :
                    ]
    total = (first[...] + partial_grad(other, cot, 1)) * SCALE
    left, right = total[:, :LANE], total[:, LANE:]
    kept[...] = jnp.where(here == 0, left, right)
    sent[...] = jnp.where(here == 0, right, left).astype(BF)
    for part, side in enumerate((left, right)):
        gate = jnp.where(here == part, query[...].astype(F32), query_pair[...].astype(F32))
        grad = (side * gate).astype(BF)
        out[:, (2 + part) * CH : (3 + part) * CH, :] = grad.reshape(HALF, CH, LANE)


def tile_of(moved, query, query_pair):
    here = lax.axis_index("h")
    parts = []
    for p in range(2):
        conv = moved[:, p * CH : (p + 1) * CH, :].reshape(WIDE, LANE).astype(F32)
        gate = jnp.where(here == p, query[...].astype(F32), query_pair[...].astype(F32))
        parts.append((gate * conv).astype(BF))
    return jnp.concatenate(parts, axis=1)


def project_kernel(moved, query, query_pair, own, other, out):
    mixed = tile_of(moved, query, query_pair).astype(F32).T.astype(BF)
    for z in range(Z):
        weight = jnp.concatenate([own[z], other[z]], axis=1)
        part = (dot(mixed, weight) * SCALE).astype(BF)
        for h in range(H):
            out[h * C + z] = part[h * LANE : (h + 1) * LANE]


def weight_kernel(moved, moved_other, query, pair, query_other, pair_other, cot, cot_other, out):
    mixed = jnp.concatenate(
        [tile_of(moved, query, pair), tile_of(moved_other, query_other, pair_other)], axis=1
    )
    for z in range(0, Z, 2):
        columns = []
        for y in (z, z + 1):
            rows = [cot[h * C + y, :, :LANE] for h in range(H)]
            rows += [cot_other[h * C + y] for h in range(H)]
            columns.append(jnp.concatenate(rows, axis=0))
        grad = dot(mixed, jnp.concatenate(columns, axis=1)) * SCALE
        out[z] = grad[:, :LANE].astype(out.dtype)
        out[z + 1] = grad[:, LANE:].astype(out.dtype)


def back_kernel(moved, spectra, first, second, second_back, twist, last, out):
    pieces = []
    for z in range(Z):
        for part in range(2):
            for k in range(K):
                low = (2 + part) * CH
                pieces.append(
                    moved[4 * z + k, low : low + CH, :].astype(F32)
                    + moved[4 * z + 2 + k, low : low + CH, :].astype(F32)
                )
    high, low = split(jnp.concatenate(pieces, axis=0))
    sides = dot(first[0], jnp.concatenate([high, low], axis=1))
    mid = sides[:, :LANE] + (sides[:, LANE:] + dot(first[1], high))
    grad = dot3(spread(mid, twist, 0), second)
    product_spec, filter_spec = spectra[:N], spectra[N:]
    both = dot3(
        jnp.concatenate([times_conj(grad, filter_spec), times_conj(grad, product_spec)], axis=0),
        second_back,
    )
    turned = jnp.concatenate([unspread(both[:N], twist), unspread(both[N:], twist)], axis=1)
    result = table_dot3(last, turned).astype(BF)
    out[:, 0:CH, :] = result[:, :LANE].reshape(HALF, CH, LANE)
    out[:, CH:, :] = result[:, LANE:].reshape(HALF, CH, LANE)


def finish_kernel(moved, key, value, key_grad, value_grad, filter_grad):
    def turned(i):
        return moved[:, i * CH : (i + 1) * CH, :].reshape(WIDE, LANE).astype(F32).T

    product_grad = turned(0)
    key_grad[...] = (product_grad * value[...].astype(F32)).astype(BF)
    value_grad[...] = (product_grad * key[...].astype(F32)).astype(BF)
    filter_grad[...] = turned(1) * (1.0 / math.sqrt(LENGTH))


def sum_kernel(parts, moved, kept, received, out, query_grad):
    k = lax.axis_index("k")
    for h in range(H):
        total = parts[h * C].astype(F32)
        for c in range(1, C):
            total = total + parts[h * C + c].astype(F32)
        total = total.astype(BF)
        for j in range(K):
            side = pl.multiple_of((2 * h + (k + j) % 2) * LANE, LANE)
            out[:, pl.ds(side, LANE)] = total[:, j * LANE : (j + 1) * LANE]
    left = moved[:, 0:CH, :].reshape(WIDE, LANE).astype(F32)
    right = moved[:, CH : 2 * CH, :].reshape(WIDE, LANE).astype(F32)
    conv = jnp.where(lax.axis_index("h") == 0, left, right)
    grad = (kept[...] + received[...].astype(F32)) * conv
    query_grad[...] = grad.T.astype(BF)


class Late:
    def __init__(self, ref, buffer, semaphore):
        self.buffer, self.copy, self.waiting = buffer, pltpu.make_async_copy(ref, buffer, semaphore), True
        self.copy.start()

    def __getitem__(self, index):
        if self.waiting:
            self.copy.wait()
            self.waiting = False
        return self.buffer[index]


class Stream:
    def __init__(self, ref, buffer, semaphores):
        self.ref, self.buffer, self.semaphores, self.copies = ref, buffer, semaphores, []
        self.dtype = ref.dtype

    def __setitem__(self, index, value):
        self.buffer[index] = value
        copy = pltpu.make_async_copy(
            self.buffer.at[index], self.ref.at[index], self.semaphores.at[len(self.copies)]
        )
        copy.start()
        self.copies.append(copy)


def call(kernel, outs, *args, flops=0, late=(), grant=GRANT, stream=False):
    shapes = tuple((pltpu.HBM if stream else jax.ShapeDtypeStruct)(s, d) for s, d in outs)
    count = len(args) + len(outs)

    def body(*refs):
        refs, rest = list(refs[:count]), list(refs[count:])
        for i, at in enumerate(late):
            refs[at] = Late(refs[at], rest[i], rest[len(late)].at[i])
        if stream:
            refs[-1] = Stream(refs[-1], rest[-2], rest[-1])
        kernel(*refs)
        for at in late:
            if refs[at].waiting:
                refs[at].copy.wait()
        if stream:
            for copy in refs[-1].copies:
                copy.wait()

    scratch = [pltpu.VMEM(args[at].shape, args[at].dtype) for at in late]
    if late:
        scratch.append(pltpu.SemaphoreType.DMA((len(late),)))
    if stream:
        scratch += [pltpu.VMEM(*outs[0]), pltpu.SemaphoreType.DMA((outs[0][0][0],))]
    out_space = pltpu.HBM if stream else pltpu.VMEM
    return pl.pallas_call(
        body,
        out_shape=shapes,
        in_specs=[
            pl.BlockSpec(memory_space=pltpu.HBM if i in late else pltpu.VMEM)
            for i in range(len(args))
        ],
        out_specs=tuple([pl.BlockSpec(memory_space=out_space)] * len(outs)),
        scratch_shapes=scratch,
        compiler_params=pltpu.CompilerParams(vmem_limit_bytes=grant),
        cost_estimate=pl.CostEstimate(flops=flops, bytes_accessed=4 << 20, transcendentals=0),
        name=kernel.__name__,
    )(*args)


def exchange(x, axes):
    return lax.all_to_all(x, axes, split_axis=0, concat_axis=0, tiled=True)


def local(queries, keys, values, filter_weight, out_weight, cotangent):
    first, second, second_back, twist, last = make_tables()
    core_pair = [(0, 1), (1, 0)]
    (packed,) = call(
        pack_kernel, [((HALF, 2 * CH, LANE), BF)], keys, values, filter_weight,
        late=(0, 1, 2), grant=FULL,
    )
    (query_t,) = call(turn_kernel, [((WIDE, LANE), BF)], queries)
    (shared,) = call(share_kernel, [((H * C, LANE, K * LANE), BF)], cotangent)
    query = (query_t, lax.ppermute(query_t, "h", core_pair))
    own = lax.all_gather(out_weight, "z")
    packed = exchange(packed, SEQ)
    packed, shared, query = lax.optimization_barrier((packed, shared, query))
    query_other = tuple(lax.ppermute(side, "k", core_pair) for side in query)
    cot = exchange(shared, PLANE)
    conv, spectra = call(
        conv_kernel,
        [((HALF * CH, LANE), BF), ((2 * N, 2 * LANE), F32)],
        packed, first, second, second_back, twist, last, flops=5_000_000_000, late=(1, 2, 3, 4, 5),
    )
    own, cot, conv = lax.optimization_barrier((own, cot, conv))
    other = lax.ppermute(own, "k", core_pair)
    own_part, side = call(
        own_grad_kernel,
        [((WIDE, H * LANE), F32), ((H * C, LANE, LANE), BF)],
        own, cot,
    )
    sent, kept, passed = call(
        grad_kernel,
        [((HALF, 4 * CH, LANE), BF), ((WIDE, LANE), F32), ((WIDE, LANE), BF)],
        own_part, other, cot, conv, *query,
    )
    cot_other = lax.ppermute(side, "k", core_pair)
    received = lax.ppermute(passed, "h", core_pair)
    moved = exchange(sent, SEQ)
    moved_other = lax.ppermute(moved, "k", core_pair)
    (out_part,) = call(project_kernel, [((H * C, LANE, K * LANE), BF)], moved, *query, own, other)
    moved_other, _ = lax.optimization_barrier((moved_other, out_part))
    (weight_part,) = call(
        weight_kernel,
        [((Z, WIDE, LANE), F32)],
        moved, moved_other, *query, *query_other, cot, cot_other, late=(7,), stream=True,
    )
    weight_grad = lax.psum_scatter(
        weight_part.reshape(Z * WIDE, LANE), "z", scatter_dimension=0, tiled=True
    )
    out_parts = exchange(out_part, PLANE)
    (back,) = call(
        back_kernel, [((HALF, 2 * CH, LANE), BF)],
        moved, spectra, first, second, second_back, twist, last, flops=8_000_000_000,
        late=(1, 2, 3, 4, 5, 6),
    )
    back, out_parts = lax.optimization_barrier((back, out_parts))
    back = exchange(back, SEQ)
    block_out, query_grad = call(
        sum_kernel,
        [((LANE, WIDE), BF), ((LANE, WIDE), BF)],
        out_parts, moved, kept, received,
    )
    key_grad, value_grad, filter_grad = call(
        finish_kernel,
        [((LANE, WIDE), BF), ((LANE, WIDE), BF), ((LANE, WIDE), F32)],
        back, keys, values,
    )
    return (block_out, query_grad, key_grad, value_grad, filter_grad, weight_grad)


def solution(mesh):
    split_mesh = Mesh(mesh.devices.reshape(Z, H, K, C), ("z", "h", "k", "chan"))
    by_position = P(SEQ, "chan")
    by_channel = P("chan", SEQ)
    in_specs = (by_position,) * 4 + (by_channel, by_position)
    out_specs = (by_position,) * 5 + (by_channel,)
    return jax.shard_map(
        local, mesh=split_mesh, in_specs=in_specs, out_specs=out_specs, check_vma=False
    )
```

```python
import functools
import math

import jax
import jax.numpy as jnp
import numpy as np
from jax import lax
from jax.experimental import pallas as pl
from jax.experimental.pallas import tpu as pltpu
from jax.sharding import Mesh
from jax.sharding import PartitionSpec as P

D = 4096
LENGTH = 4096
PADDED = 2 * LENGTH
LANE = 128
OUTER = PADDED // LANE
HALF = OUTER // 2
ROWS = HALF + 1
CH = 16
WIDE = 512
Z, H, K, C = 8, 2, 2, 8
SEQ = ("z", "h", "k")
PLANE = ("h", "chan")
BF = jnp.bfloat16
F32 = jnp.float32
SCALE = 1.0 / math.sqrt(D)
GRANT = 40 * 1024 * 1024
FULL = 64 * 1024 * 1024


def halves(table):
    high = np.asarray(table, np.float32).astype(BF)
    low = (np.asarray(table, np.float64) - high.astype(np.float64)).astype(np.float32).astype(BF)
    return np.stack([high, low])


@functools.lru_cache(maxsize=1)
def make_tables():
    outer = np.arange(ROWS)[:, None] * np.arange(HALF)[None, :] % OUTER
    angle = -2.0 * np.pi / OUTER * outer
    eye = np.eye(CH)
    first = np.concatenate([np.kron(np.cos(angle), eye), np.kron(np.sin(angle), eye)], axis=0)
    inner = np.arange(LANE)[:, None] * np.arange(LANE)[None, :] % LANE
    inner_cos = np.cos(2.0 * np.pi / LANE * inner)
    inner_sin = np.sin(-2.0 * np.pi / LANE * inner)
    second = np.block([[inner_cos, inner_sin], [-inner_sin, inner_cos]])
    turn = -2.0 * np.pi / PADDED * (np.arange(ROWS)[:, None] * np.arange(LANE)[None, :])
    turn = np.repeat(turn, CH, axis=0)
    twist = np.stack([np.cos(turn), np.sin(turn)]).astype(np.float32)
    count = np.full((ROWS,), 2.0)
    count[0] = count[-1] = 1.0
    back = count[None, :] / PADDED
    last = np.concatenate(
        [np.kron(np.cos(angle).T * back, eye), np.kron(np.sin(angle).T * back, eye)], axis=1
    )
    return (halves(first), halves(second), halves(second.T), twist, halves(last))


def split(x):
    high = x.astype(BF)
    return high, (x - high.astype(F32)).astype(BF)


def dot(a, b):
    return jnp.dot(a, b, preferred_element_type=F32)


def dot3(a, table):
    high, low = split(a)
    return dot(high, table[0]) + (dot(low, table[0]) + dot(high, table[1]))


def table_dot3(table, b):
    high, low = split(b)
    return dot(table[0], high) + (dot(table[0], low) + dot(table[1], high))


N = ROWS * CH


def spread(mid, twist, col):
    real = mid[:N, col : col + LANE]
    imag = mid[N:, col : col + LANE]
    return jnp.concatenate(
        [real * twist[0] - imag * twist[1], real * twist[1] + imag * twist[0]], axis=1
    )


def unspread(mid, twist):
    real = mid[:, :LANE]
    imag = mid[:, LANE:]
    return jnp.concatenate(
        [real * twist[0] + imag * twist[1], imag * twist[0] - real * twist[1]], axis=0
    )


def times(a, b):
    ar, ai, br, bi = a[:, :LANE], a[:, LANE:], b[:, :LANE], b[:, LANE:]
    return jnp.concatenate([ar * br - ai * bi, ar * bi + ai * br], axis=1)


def times_conj(a, b):
    ar, ai, br, bi = a[:, :LANE], a[:, LANE:], b[:, :LANE], b[:, LANE:]
    return jnp.concatenate([ar * br + ai * bi, ai * br - ar * bi], axis=1)


def pack_kernel(key, value, weight, out):
    product = key[...].astype(F32) * value[...].astype(F32)
    for i, signal in enumerate((product, weight[...] * (1.0 / math.sqrt(LENGTH)))):
        out[:, i * CH : (i + 1) * CH, :] = signal.T.astype(BF).reshape(HALF, CH, LANE)


def turn_kernel(query, out):
    out[...] = query[...].astype(F32).T.astype(BF)


def share_kernel(cot, out):
    k = lax.axis_index("k")
    for h in range(H):
        for j in range(K):
            side = pl.multiple_of((2 * h + (k + j) % 2) * LANE, LANE)
            piece = cot[:, pl.ds(side, LANE)]
            for c in range(C):
                out[h * C + c, :, j * LANE : (j + 1) * LANE] = piece


def conv_kernel(packed, first, second, second_back, twist, last, conv, spectra):
    product = packed[:, 0:CH, :].reshape(HALF * CH, LANE)
    weight = packed[:, CH:, :].reshape(HALF * CH, LANE)
    both = jnp.concatenate([product, weight], axis=1)
    mid = dot(first[0], both) + dot(first[1], both)
    spec = dot3(
        jnp.concatenate([spread(mid, twist, 0), spread(mid, twist, LANE)], axis=0), second
    )
    spectra[...] = spec
    turned = unspread(dot3(times(spec[:N], spec[N:]), second_back), twist)
    conv[...] = table_dot3(last, turned).astype(BF)


def partial_grad(weights, cot, side):
    total = jnp.zeros((WIDE, H * LANE), F32)
    columns = slice(side * LANE, (side + 1) * LANE)
    for z in range(0, Z, 2):
        weight = jnp.concatenate([weights[z], weights[z + 1]], axis=1)
        rows = [
            jnp.concatenate([cot[h * C + z, :, columns], cot[h * C + z + 1, :, columns]], axis=1)
            for h in range(H)
        ]
        total = total + lax.dot_general(
            weight,
            jnp.concatenate(rows, axis=0),
            (((1,), (1,)), ((), ())),
            preferred_element_type=F32,
        )
    return total


def own_grad_kernel(own, cot, out, side):
    side[...] = cot[:, :, LANE:]
    out[...] = partial_grad(own, cot, 0)


def grad_kernel(first, other, cot, conv, query, query_pair, out, kept, sent):
    here = lax.axis_index("h")
    for z in range(Z):
        for h in range(H):
            for k in range(K):
                for part in range(2):
                    a = 4 * z + 2 * part + k
                    out[4 * z + 2 * h + k, part * CH : (part + 1) * CH, :] = conv[
                        a * CH : (a + 1) * CH, :
                    ]
    total = (first[...] + partial_grad(other, cot, 1)) * SCALE
    left, right = total[:, :LANE], total[:, LANE:]
    kept[...] = jnp.where(here == 0, left, right)
    sent[...] = jnp.where(here == 0, right, left).astype(BF)
    for part, side in enumerate((left, right)):
        gate = jnp.where(here == part, query[...].astype(F32), query_pair[...].astype(F32))
        grad = (side * gate).astype(BF)
        out[:, (2 + part) * CH : (3 + part) * CH, :] = grad.reshape(HALF, CH, LANE)


def tile_of(moved, query, query_pair):
    here = lax.axis_index("h")
    parts = []
    for p in range(2):
        conv = moved[:, p * CH : (p + 1) * CH, :].reshape(WIDE, LANE).astype(F32)
        gate = jnp.where(here == p, query[...].astype(F32), query_pair[...].astype(F32))
        parts.append((gate * conv).astype(BF))
    return jnp.concatenate(parts, axis=1)


def project_kernel(moved, query, query_pair, own, other, out):
    mixed = tile_of(moved, query, query_pair).astype(F32).T.astype(BF)
    for z in range(Z):
        weight = jnp.concatenate([own[z], other[z]], axis=1)
        part = (dot(mixed, weight) * SCALE).astype(BF)
        for h in range(H):
            out[h * C + z] = part[h * LANE : (h + 1) * LANE]


def weight_kernel(moved, moved_other, query, pair, query_other, pair_other, cot, cot_other, out):
    mixed = jnp.concatenate(
        [tile_of(moved, query, pair), tile_of(moved_other, query_other, pair_other)], axis=1
    )
    for z in range(0, Z, 2):
        columns = []
        for y in (z, z + 1):
            rows = [cot[h * C + y, :, :LANE] for h in range(H)]
            rows += [cot_other[h * C + y] for h in range(H)]
            columns.append(jnp.concatenate(rows, axis=0))
        grad = dot(mixed, jnp.concatenate(columns, axis=1)) * SCALE
        out[z] = grad[:, :LANE].astype(out.dtype)
        out[z + 1] = grad[:, LANE:].astype(out.dtype)


def back_kernel(moved, spectra, first, second, second_back, twist, last, out):
    pieces = []
    for z in range(Z):
        for part in range(2):
            for k in range(K):
                low = (2 + part) * CH
                pieces.append(
                    moved[4 * z + k, low : low + CH, :].astype(F32)
                    + moved[4 * z + 2 + k, low : low + CH, :].astype(F32)
                )
    high, low = split(jnp.concatenate(pieces, axis=0))
    sides = dot(first[0], jnp.concatenate([high, low], axis=1))
    mid = sides[:, :LANE] + (sides[:, LANE:] + dot(first[1], high))
    grad = dot3(spread(mid, twist, 0), second)
    product_spec, filter_spec = spectra[:N], spectra[N:]
    both = dot3(
        jnp.concatenate([times_conj(grad, filter_spec), times_conj(grad, product_spec)], axis=0),
        second_back,
    )
    turned = jnp.concatenate([unspread(both[:N], twist), unspread(both[N:], twist)], axis=1)
    result = table_dot3(last, turned).astype(BF)
    out[:, 0:CH, :] = result[:, :LANE].reshape(HALF, CH, LANE)
    out[:, CH:, :] = result[:, LANE:].reshape(HALF, CH, LANE)


def finish_kernel(moved, key, value, key_grad, value_grad, filter_grad):
    def turned(i):
        return moved[:, i * CH : (i + 1) * CH, :].reshape(WIDE, LANE).astype(F32).T

    product_grad = turned(0)
    key_grad[...] = (product_grad * value[...].astype(F32)).astype(BF)
    value_grad[...] = (product_grad * key[...].astype(F32)).astype(BF)
    filter_grad[...] = turned(1) * (1.0 / math.sqrt(LENGTH))


def sum_kernel(parts, moved, kept, received, out, query_grad):
    k = lax.axis_index("k")
    for h in range(H):
        total = parts[h * C].astype(F32)
        for c in range(1, C):
            total = total + parts[h * C + c].astype(F32)
        total = total.astype(BF)
        for j in range(K):
            side = pl.multiple_of((2 * h + (k + j) % 2) * LANE, LANE)
            out[:, pl.ds(side, LANE)] = total[:, j * LANE : (j + 1) * LANE]
    left = moved[:, 0:CH, :].reshape(WIDE, LANE).astype(F32)
    right = moved[:, CH : 2 * CH, :].reshape(WIDE, LANE).astype(F32)
    conv = jnp.where(lax.axis_index("h") == 0, left, right)
    grad = (kept[...] + received[...].astype(F32)) * conv
    query_grad[...] = grad.T.astype(BF)


class Late:
    def __init__(self, ref, buffer, semaphore):
        self.buffer, self.copy, self.waiting = buffer, pltpu.make_async_copy(ref, buffer, semaphore), True
        self.copy.start()

    def __getitem__(self, index):
        if self.waiting:
            self.copy.wait()
            self.waiting = False
        return self.buffer[index]


class Stream:
    def __init__(self, ref, buffer, semaphores):
        self.ref, self.buffer, self.semaphores, self.copies = ref, buffer, semaphores, []
        self.dtype = ref.dtype

    def __setitem__(self, index, value):
        self.buffer[index] = value
        copy = pltpu.make_async_copy(
            self.buffer.at[index], self.ref.at[index], self.semaphores.at[len(self.copies)]
        )
        copy.start()
        self.copies.append(copy)


def call(kernel, outs, *args, flops=0, late=(), grant=GRANT, stream=False):
    shapes = tuple((pltpu.HBM if stream else jax.ShapeDtypeStruct)(s, d) for s, d in outs)
    count = len(args) + len(outs)

    def body(*refs):
        refs, rest = list(refs[:count]), list(refs[count:])
        for i, at in enumerate(late):
            refs[at] = Late(refs[at], rest[i], rest[len(late)].at[i])
        if stream:
            refs[-1] = Stream(refs[-1], rest[-2], rest[-1])
        kernel(*refs)
        for at in late:
            if refs[at].waiting:
                refs[at].copy.wait()
        if stream:
            for copy in refs[-1].copies:
                copy.wait()

    scratch = [pltpu.VMEM(args[at].shape, args[at].dtype) for at in late]
    if late:
        scratch.append(pltpu.SemaphoreType.DMA((len(late),)))
    if stream:
        scratch += [pltpu.VMEM(*outs[0]), pltpu.SemaphoreType.DMA((outs[0][0][0],))]
    out_space = pltpu.HBM if stream else pltpu.VMEM
    return pl.pallas_call(
        body,
        out_shape=shapes,
        in_specs=[
            pl.BlockSpec(memory_space=pltpu.HBM if i in late else pltpu.VMEM)
            for i in range(len(args))
        ],
        out_specs=tuple([pl.BlockSpec(memory_space=out_space)] * len(outs)),
        scratch_shapes=scratch,
        compiler_params=pltpu.CompilerParams(vmem_limit_bytes=grant),
        cost_estimate=pl.CostEstimate(flops=flops, bytes_accessed=4 << 20, transcendentals=0),
        name=kernel.__name__,
    )(*args)


def exchange(x, axes):
    return lax.all_to_all(x, axes, split_axis=0, concat_axis=0, tiled=True)


def local(queries, keys, values, filter_weight, out_weight, cotangent):
    first, second, second_back, twist, last = make_tables()
    core_pair = [(0, 1), (1, 0)]
    (packed,) = call(
        pack_kernel, [((HALF, 2 * CH, LANE), BF)], keys, values, filter_weight,
        late=(0, 1, 2), grant=FULL, stream=True,
    )
    (query_t,) = call(turn_kernel, [((WIDE, LANE), BF)], queries)
    (shared,) = call(share_kernel, [((H * C, LANE, K * LANE), BF)], cotangent)
    query = (query_t, lax.ppermute(query_t, "h", core_pair))
    own = lax.all_gather(out_weight, "z")
    packed = exchange(packed, SEQ)
    packed, shared, query = lax.optimization_barrier((packed, shared, query))
    query_other = tuple(lax.ppermute(side, "k", core_pair) for side in query)
    cot = exchange(shared, PLANE)
    conv, spectra = call(
        conv_kernel,
        [((HALF * CH, LANE), BF), ((2 * N, 2 * LANE), F32)],
        packed, first, second, second_back, twist, last, flops=5_000_000_000, late=(1, 2, 3, 4, 5),
    )
    own, cot, conv = lax.optimization_barrier((own, cot, conv))
    other = lax.ppermute(own, "k", core_pair)
    own_part, side = call(
        own_grad_kernel,
        [((WIDE, H * LANE), F32), ((H * C, LANE, LANE), BF)],
        own, cot,
    )
    sent, kept, passed = call(
        grad_kernel,
        [((HALF, 4 * CH, LANE), BF), ((WIDE, LANE), F32), ((WIDE, LANE), BF)],
        own_part, other, cot, conv, *query,
    )
    cot_other = lax.ppermute(side, "k", core_pair)
    received = lax.ppermute(passed, "h", core_pair)
    moved = exchange(sent, SEQ)
    moved_other = lax.ppermute(moved, "k", core_pair)
    (out_part,) = call(project_kernel, [((H * C, LANE, K * LANE), BF)], moved, *query, own, other, stream=True)
    moved_other, _ = lax.optimization_barrier((moved_other, out_part))
    (weight_part,) = call(
        weight_kernel,
        [((Z, WIDE, LANE), F32)],
        moved, moved_other, *query, *query_other, cot, cot_other, late=(7,), stream=True,
    )
    weight_grad = lax.psum_scatter(
        weight_part.reshape(Z * WIDE, LANE), "z", scatter_dimension=0, tiled=True
    )
    out_parts = exchange(out_part, PLANE)
    (back,) = call(
        back_kernel, [((HALF, 2 * CH, LANE), BF)],
        moved, spectra, first, second, second_back, twist, last, flops=8_000_000_000,
        late=(1, 2, 3, 4, 5, 6),
    )
    back, out_parts = lax.optimization_barrier((back, out_parts))
    back = exchange(back, SEQ)
    block_out, query_grad = call(
        sum_kernel,
        [((LANE, WIDE), BF), ((LANE, WIDE), BF)],
        out_parts, moved, kept, received,
    )
    key_grad, value_grad, filter_grad = call(
        finish_kernel,
        [((LANE, WIDE), BF), ((LANE, WIDE), BF), ((LANE, WIDE), F32)],
        back, keys, values,
    )
    return (block_out, query_grad, key_grad, value_grad, filter_grad, weight_grad)


def solution(mesh):
    split_mesh = Mesh(mesh.devices.reshape(Z, H, K, C), ("z", "h", "k", "chan"))
    by_position = P(SEQ, "chan")
    by_channel = P("chan", SEQ)
    in_specs = (by_position,) * 4 + (by_channel, by_position)
    out_specs = (by_position,) * 5 + (by_channel,)
    return jax.shard_map(
        local, mesh=split_mesh, in_specs=in_specs, out_specs=out_specs, check_vma=False
    )
```

```python
import functools
import math

import jax
import jax.numpy as jnp
import numpy as np
from jax import lax
from jax.experimental import pallas as pl
from jax.experimental.pallas import tpu as pltpu
from jax.sharding import Mesh
from jax.sharding import PartitionSpec as P

D = 4096
LENGTH = 4096
PADDED = 2 * LENGTH
LANE = 128
OUTER = PADDED // LANE
HALF = OUTER // 2
ROWS = HALF + 1
CH = 16
WIDE = 512
Z, H, K, C = 8, 2, 2, 8
SEQ = ("z", "h", "k")
PLANE = ("h", "chan")
BF = jnp.bfloat16
F32 = jnp.float32
SCALE = 1.0 / math.sqrt(D)
GRANT = 40 * 1024 * 1024
FULL = 64 * 1024 * 1024


def halves(table):
    high = np.asarray(table, np.float32).astype(BF)
    low = (np.asarray(table, np.float64) - high.astype(np.float64)).astype(np.float32).astype(BF)
    return np.stack([high, low])


@functools.lru_cache(maxsize=1)
def make_tables():
    outer = np.arange(ROWS)[:, None] * np.arange(HALF)[None, :] % OUTER
    angle = -2.0 * np.pi / OUTER * outer
    eye = np.eye(CH)
    first = np.concatenate([np.kron(np.cos(angle), eye), np.kron(np.sin(angle), eye)], axis=0)
    inner = np.arange(LANE)[:, None] * np.arange(LANE)[None, :] % LANE
    inner_cos = np.cos(2.0 * np.pi / LANE * inner)
    inner_sin = np.sin(-2.0 * np.pi / LANE * inner)
    second = np.block([[inner_cos, inner_sin], [-inner_sin, inner_cos]])
    turn = -2.0 * np.pi / PADDED * (np.arange(ROWS)[:, None] * np.arange(LANE)[None, :])
    turn = np.repeat(turn, CH, axis=0)
    twist = np.stack([np.cos(turn), np.sin(turn)]).astype(np.float32)
    count = np.full((ROWS,), 2.0)
    count[0] = count[-1] = 1.0
    back = count[None, :] / PADDED
    last = np.concatenate(
        [np.kron(np.cos(angle).T * back, eye), np.kron(np.sin(angle).T * back, eye)], axis=1
    )
    return (halves(first), halves(second), halves(second.T), twist, halves(last))


def split(x):
    high = x.astype(BF)
    return high, (x - high.astype(F32)).astype(BF)


def dot(a, b):
    return jnp.dot(a, b, preferred_element_type=F32)


def dot3(a, table):
    high, low = split(a)
    return dot(high, table[0]) + (dot(low, table[0]) + dot(high, table[1]))


def table_dot3(table, b):
    high, low = split(b)
    return dot(table[0], high) + (dot(table[0], low) + dot(table[1], high))


N = ROWS * CH


def spread(mid, twist, col):
    real = mid[:N, col : col + LANE]
    imag = mid[N:, col : col + LANE]
    return jnp.concatenate(
        [real * twist[0] - imag * twist[1], real * twist[1] + imag * twist[0]], axis=1
    )


def unspread(mid, twist):
    real = mid[:, :LANE]
    imag = mid[:, LANE:]
    return jnp.concatenate(
        [real * twist[0] + imag * twist[1], imag * twist[0] - real * twist[1]], axis=0
    )


def times(a, b):
    ar, ai, br, bi = a[:, :LANE], a[:, LANE:], b[:, :LANE], b[:, LANE:]
    return jnp.concatenate([ar * br - ai * bi, ar * bi + ai * br], axis=1)


def times_conj(a, b):
    ar, ai, br, bi = a[:, :LANE], a[:, LANE:], b[:, :LANE], b[:, LANE:]
    return jnp.concatenate([ar * br + ai * bi, ai * br - ar * bi], axis=1)


def pack_kernel(key, value, weight, out):
    product = key[...].astype(F32) * value[...].astype(F32)
    for i, signal in enumerate((product, weight[...] * (1.0 / math.sqrt(LENGTH)))):
        out[:, i * CH : (i + 1) * CH, :] = signal.T.astype(BF).reshape(HALF, CH, LANE)


def turn_kernel(query, out):
    out[...] = query[...].astype(F32).T.astype(BF)


def share_kernel(cot, out):
    k = lax.axis_index("k")
    for h in range(H):
        for j in range(K):
            side = pl.multiple_of((2 * h + (k + j) % 2) * LANE, LANE)
            piece = cot[:, pl.ds(side, LANE)]
            for c in range(C):
                out[h * C + c, :, j * LANE : (j + 1) * LANE] = piece


def conv_kernel(packed, first, second, second_back, twist, last, conv, spectra):
    product = packed[:, 0:CH, :].reshape(HALF * CH, LANE)
    weight = packed[:, CH:, :].reshape(HALF * CH, LANE)
    both = jnp.concatenate([product, weight], axis=1)
    mid = dot(first[0], both) + dot(first[1], both)
    spec = dot3(
        jnp.concatenate([spread(mid, twist, 0), spread(mid, twist, LANE)], axis=0), second
    )
    spectra[...] = spec
    turned = unspread(dot3(times(spec[:N], spec[N:]), second_back), twist)
    conv[...] = table_dot3(last, turned).astype(BF)


def partial_grad(weights, cot, side):
    total = jnp.zeros((WIDE, H * LANE), F32)
    columns = slice(side * LANE, (side + 1) * LANE)
    for z in range(0, Z, 2):
        weight = jnp.concatenate([weights[z], weights[z + 1]], axis=1)
        rows = [
            jnp.concatenate([cot[h * C + z, :, columns], cot[h * C + z + 1, :, columns]], axis=1)
            for h in range(H)
        ]
        total = total + lax.dot_general(
            weight,
            jnp.concatenate(rows, axis=0),
            (((1,), (1,)), ((), ())),
            preferred_element_type=F32,
        )
    return total


def own_grad_kernel(own, cot, out, side):
    side[...] = cot[:, :, LANE:]
    out[...] = partial_grad(own, cot, 0)


def grad_kernel(first, other, cot, conv, query, query_pair, out, kept, sent):
    here = lax.axis_index("h")
    for z in range(Z):
        for h in range(H):
            for k in range(K):
                for part in range(2):
                    a = 4 * z + 2 * part + k
                    out[4 * z + 2 * h + k, part * CH : (part + 1) * CH, :] = conv[
                        a * CH : (a + 1) * CH, :
                    ]
    total = (first[...] + partial_grad(other, cot, 1)) * SCALE
    left, right = total[:, :LANE], total[:, LANE:]
    kept[...] = jnp.where(here == 0, left, right)
    sent[...] = jnp.where(here == 0, right, left).astype(BF)
    for part, side in enumerate((left, right)):
        gate = jnp.where(here == part, query[...].astype(F32), query_pair[...].astype(F32))
        grad = (side * gate).astype(BF)
        out[:, (2 + part) * CH : (3 + part) * CH, :] = grad.reshape(HALF, CH, LANE)


def tile_of(moved, query, query_pair):
    here = lax.axis_index("h")
    parts = []
    for p in range(2):
        conv = moved[:, p * CH : (p + 1) * CH, :].reshape(WIDE, LANE).astype(F32)
        gate = jnp.where(here == p, query[...].astype(F32), query_pair[...].astype(F32))
        parts.append((gate * conv).astype(BF))
    return jnp.concatenate(parts, axis=1)


def project_kernel(moved, query, query_pair, own, other, out):
    mixed = tile_of(moved, query, query_pair).astype(F32).T.astype(BF)
    for z in range(Z):
        weight = jnp.concatenate([own[z], other[z]], axis=1)
        part = (dot(mixed, weight) * SCALE).astype(BF)
        for h in range(H):
            out[h * C + z] = part[h * LANE : (h + 1) * LANE]


def weight_kernel(moved, moved_other, query, pair, query_other, pair_other, cot, cot_other, out):
    mixed = jnp.concatenate(
        [tile_of(moved, query, pair), tile_of(moved_other, query_other, pair_other)], axis=1
    )
    for z in range(0, Z, 2):
        columns = []
        for y in (z, z + 1):
            rows = [cot[h * C + y, :, :LANE] for h in range(H)]
            rows += [cot_other[h * C + y] for h in range(H)]
            columns.append(jnp.concatenate(rows, axis=0))
        grad = dot(mixed, jnp.concatenate(columns, axis=1)) * SCALE
        out[z] = grad[:, :LANE].astype(out.dtype)
        out[z + 1] = grad[:, LANE:].astype(out.dtype)


def back_kernel(moved, spectra, first, second, second_back, twist, last, out):
    pieces = []
    for z in range(Z):
        for part in range(2):
            for k in range(K):
                low = (2 + part) * CH
                pieces.append(
                    moved[4 * z + k, low : low + CH, :].astype(F32)
                    + moved[4 * z + 2 + k, low : low + CH, :].astype(F32)
                )
    high, low = split(jnp.concatenate(pieces, axis=0))
    sides = dot(first[0], jnp.concatenate([high, low], axis=1))
    mid = sides[:, :LANE] + (sides[:, LANE:] + dot(first[1], high))
    grad = dot3(spread(mid, twist, 0), second)
    product_spec, filter_spec = spectra[:N], spectra[N:]
    both = dot3(
        jnp.concatenate([times_conj(grad, filter_spec), times_conj(grad, product_spec)], axis=0),
        second_back,
    )
    turned = jnp.concatenate([unspread(both[:N], twist), unspread(both[N:], twist)], axis=1)
    result = table_dot3(last, turned).astype(BF)
    out[:, 0:CH, :] = result[:, :LANE].reshape(HALF, CH, LANE)
    out[:, CH:, :] = result[:, LANE:].reshape(HALF, CH, LANE)


def finish_kernel(moved, key, value, key_grad, value_grad, filter_grad):
    def turned(i):
        return moved[:, i * CH : (i + 1) * CH, :].reshape(WIDE, LANE).astype(F32).T

    product_grad = turned(0)
    key_grad[...] = (product_grad * value[...].astype(F32)).astype(BF)
    value_grad[...] = (product_grad * key[...].astype(F32)).astype(BF)
    filter_grad[...] = turned(1) * (1.0 / math.sqrt(LENGTH))


def sum_kernel(parts, moved, kept, received, out, query_grad):
    k = lax.axis_index("k")
    for h in range(H):
        total = parts[h * C].astype(F32)
        for c in range(1, C):
            total = total + parts[h * C + c].astype(F32)
        total = total.astype(BF)
        for j in range(K):
            side = pl.multiple_of((2 * h + (k + j) % 2) * LANE, LANE)
            out[:, pl.ds(side, LANE)] = total[:, j * LANE : (j + 1) * LANE]
    left = moved[:, 0:CH, :].reshape(WIDE, LANE).astype(F32)
    right = moved[:, CH : 2 * CH, :].reshape(WIDE, LANE).astype(F32)
    conv = jnp.where(lax.axis_index("h") == 0, left, right)
    grad = (kept[...] + received[...].astype(F32)) * conv
    query_grad[...] = grad.T.astype(BF)


class Late:
    def __init__(self, ref, buffer, semaphore):
        self.buffer, self.copy, self.waiting = buffer, pltpu.make_async_copy(ref, buffer, semaphore), True
        self.copy.start()

    def __getitem__(self, index):
        if self.waiting:
            self.copy.wait()
            self.waiting = False
        return self.buffer[index]


class Stream:
    def __init__(self, ref, buffer, semaphores):
        self.ref, self.buffer, self.semaphores, self.copies = ref, buffer, semaphores, []
        self.dtype = ref.dtype

    def __setitem__(self, index, value):
        self.buffer[index] = value
        copy = pltpu.make_async_copy(
            self.buffer.at[index], self.ref.at[index], self.semaphores.at[len(self.copies)]
        )
        copy.start()
        self.copies.append(copy)


def call(kernel, outs, *args, flops=0, late=(), grant=GRANT, stream=False):
    shapes = tuple((pltpu.HBM if stream else jax.ShapeDtypeStruct)(s, d) for s, d in outs)
    count = len(args) + len(outs)

    def body(*refs):
        refs, rest = list(refs[:count]), list(refs[count:])
        for i, at in enumerate(late):
            refs[at] = Late(refs[at], rest[i], rest[len(late)].at[i])
        if stream:
            refs[-1] = Stream(refs[-1], rest[-2], rest[-1])
        kernel(*refs)
        for at in late:
            if refs[at].waiting:
                refs[at].copy.wait()
        if stream:
            for copy in refs[-1].copies:
                copy.wait()

    scratch = [pltpu.VMEM(args[at].shape, args[at].dtype) for at in late]
    if late:
        scratch.append(pltpu.SemaphoreType.DMA((len(late),)))
    if stream:
        scratch += [pltpu.VMEM(*outs[0]), pltpu.SemaphoreType.DMA((outs[0][0][0],))]
    out_space = pltpu.HBM if stream else pltpu.VMEM
    return pl.pallas_call(
        body,
        out_shape=shapes,
        in_specs=[
            pl.BlockSpec(memory_space=pltpu.HBM if i in late else pltpu.VMEM)
            for i in range(len(args))
        ],
        out_specs=tuple([pl.BlockSpec(memory_space=out_space)] * len(outs)),
        scratch_shapes=scratch,
        compiler_params=pltpu.CompilerParams(vmem_limit_bytes=grant),
        cost_estimate=pl.CostEstimate(flops=flops, bytes_accessed=4 << 20, transcendentals=0),
        name=kernel.__name__,
    )(*args)


def exchange(x, axes):
    return lax.all_to_all(x, axes, split_axis=0, concat_axis=0, tiled=True)


def local(queries, keys, values, filter_weight, out_weight, cotangent):
    first, second, second_back, twist, last = make_tables()
    core_pair = [(0, 1), (1, 0)]
    (packed,) = call(
        pack_kernel, [((HALF, 2 * CH, LANE), BF)], keys, values, filter_weight,
        late=(0, 1, 2), grant=FULL,
    )
    (query_t,) = call(turn_kernel, [((WIDE, LANE), BF)], queries)
    (shared,) = call(share_kernel, [((H * C, LANE, K * LANE), BF)], cotangent)
    query = (query_t, lax.ppermute(query_t, "h", core_pair))
    own = lax.all_gather(out_weight, "z")
    packed = exchange(packed, SEQ)
    packed, shared, query = lax.optimization_barrier((packed, shared, query))
    query_other = tuple(lax.ppermute(side, "k", core_pair) for side in query)
    cot = exchange(shared, PLANE)
    conv, spectra = call(
        conv_kernel,
        [((HALF * CH, LANE), BF), ((2 * N, 2 * LANE), F32)],
        packed, first, second, second_back, twist, last, flops=5_000_000_000, late=(1, 2, 3, 4, 5),
    )
    own, cot, conv, query_other = lax.optimization_barrier((own, cot, conv, query_other))
    other = lax.ppermute(own, "k", core_pair)
    own_part, side = call(
        own_grad_kernel,
        [((WIDE, H * LANE), F32), ((H * C, LANE, LANE), BF)],
        own, cot,
    )
    sent, kept, passed = call(
        grad_kernel,
        [((HALF, 4 * CH, LANE), BF), ((WIDE, LANE), F32), ((WIDE, LANE), BF)],
        own_part, other, cot, conv, *query,
    )
    cot_other = lax.ppermute(side, "k", core_pair)
    received = lax.ppermute(passed, "h", core_pair)
    moved = exchange(sent, SEQ)
    moved_other = lax.ppermute(moved, "k", core_pair)
    (out_part,) = call(project_kernel, [((H * C, LANE, K * LANE), BF)], moved, *query, own, other)
    moved_other, _ = lax.optimization_barrier((moved_other, out_part))
    (weight_part,) = call(
        weight_kernel,
        [((Z, WIDE, LANE), F32)],
        moved, moved_other, *query, *query_other, cot, cot_other, late=(7,), stream=True,
    )
    weight_grad = lax.psum_scatter(
        weight_part.reshape(Z * WIDE, LANE), "z", scatter_dimension=0, tiled=True
    )
    out_parts = exchange(out_part, PLANE)
    (back,) = call(
        back_kernel, [((HALF, 2 * CH, LANE), BF)],
        moved, spectra, first, second, second_back, twist, last, flops=8_000_000_000,
        late=(1, 2, 3, 4, 5, 6),
    )
    back, out_parts = lax.optimization_barrier((back, out_parts))
    back = exchange(back, SEQ)
    block_out, query_grad = call(
        sum_kernel,
        [((LANE, WIDE), BF), ((LANE, WIDE), BF)],
        out_parts, moved, kept, received,
    )
    key_grad, value_grad, filter_grad = call(
        finish_kernel,
        [((LANE, WIDE), BF), ((LANE, WIDE), BF), ((LANE, WIDE), F32)],
        back, keys, values,
    )
    return (block_out, query_grad, key_grad, value_grad, filter_grad, weight_grad)


def solution(mesh):
    split_mesh = Mesh(mesh.devices.reshape(Z, H, K, C), ("z", "h", "k", "chan"))
    by_position = P(SEQ, "chan")
    by_channel = P("chan", SEQ)
    in_specs = (by_position,) * 4 + (by_channel, by_position)
    out_specs = (by_position,) * 5 + (by_channel,)
    return jax.shard_map(
        local, mesh=split_mesh, in_specs=in_specs, out_specs=out_specs, check_vma=False
    )
```
